32 devices in a mesh: dp: 4 (over y, core), cuts: 8 (over z, x).
Axes of the slice: x: 2, y: 2, z: 4, core: 2. Of those that a mesh axis runs over, the one named last changes fastest.
Arguments:
- hidden: bfloat16 [4, 256, 8192], P('dp', None, 'cuts'), may hold values from -6 to 6
- down_weight: bfloat16 [4, 8192, 3072], P('dp', 'cuts'), may hold values from -0.0625 to 0.0625
- expert_ids: int32 [512, 2], P('dp'), may hold values from 0 to 7, all different within a row; in each aligned block of 128 rows (0 to 127, 128 to 255, ...) at most 64 rows name the same one
- combine: float32 [512, 2], P('dp'), may hold values from 0.1 to 1
- out_grad: bfloat16 [512, 3072], P('dp', 'cuts'), may hold values from -6 to 6
Outputs:
- mixed: bfloat16 [512, 3072], P('dp', 'cuts')
- hidden_grad: bfloat16 [4, 256, 8192], P('dp', None, 'cuts')
- weight_grad: bfloat16 [4, 8192, 3072], P('dp', 'cuts')
The draws below stay inside these ranges and needn't reach their ends.
Inputs may be any that keep to these rules, and one draw needn't show every extreme that they name: `expert_ids`: the two ids of a row differ. Among the 256 pairs of one index of dp, no expert is named more than 64 times, a bound that some block reaches.
All inputs are finite; a program needn't handle non-finite values.
Results may differ from the reference program's by a relative error of at most 0.0049.
Values may be sent and summed in bfloat16 or wider, within the bound.
No kernel may reach another device: no remote copies, remote signals or barrier semaphores. Data moves between devices by JAX's collectives and lax.ppermute only.
A program may use at most 64 MiB of HBM per device.

```python
import math
import jax
import jax.numpy as jnp
import numpy as np
from jax import lax

D = 3072
FF = 8192
T_DP = 128
TOKENS = 512
EXPERTS = 8
WINDOW = 4
CAP = 64
SLOTS = 256
N_DP = 4


def block_scale(rng, shape, split, low, top_value):
    level, own = 1.0, jax.random.fold_in(rng, 6)
    for position, parts in split:
        draws = jnp.exp(jax.random.uniform(jax.random.fold_in(own, position), (parts,), jnp.float32, low / len(split), top_value / len(split)))
        level = level * jnp.repeat(draws, shape[position] // parts).reshape([-1 if axis == position else 1 for axis in range(len(shape))])
    return level


def assign_block(stream_key, own, number, rows, amount, top, limit, slope):
    sequence = jax.random.permutation(stream_key, amount)
    crowded, common = load_shares(amount, rows * top, limit, slope, True), load_shares(amount, rows * top, limit, slope, False)
    places = jnp.arange(amount)

    def named(sizes, offset_by):
        used = int((sizes > 0).sum())
        fixed = max(1, used // 4)
        moved = fixed + (places - fixed + offset_by * (used - fixed)) % max(1, amount - fixed)
        return jnp.zeros((amount,), jnp.int32).at[sequence[jnp.where(places < fixed, places, moved)]].set(jnp.asarray(sizes, jnp.int32))

    sizes = jnp.where(number % 4 == 0, named(crowded, number // 4), named(common, number - number // 4 - 1))
    mixed = jax.random.permutation(jax.random.fold_in(own, 3), amount)
    source_of, receiver = mixed[0:amount // 2 * 2:2], mixed[1:amount // 2 * 2:2]
    margin = jnp.minimum(sizes[source_of] - 1, limit - sizes[receiver]) // 2
    margin = jnp.where((source_of == sequence[0]) | (receiver == sequence[0]) | (sizes[receiver] == 0), 0, jnp.maximum(margin, 0))
    moved = jax.random.randint(jax.random.fold_in(own, 4), (amount // 2,), 0, 1 << 20) % (margin + 1)
    sizes = sizes.at[source_of].add(-moved).at[receiver].add(moved)
    members = jnp.searchsorted(jnp.cumsum(sizes), jnp.arange(rows * top), side="right").astype(jnp.int32)
    listing = members.reshape(top, rows).T
    listing = listing[jax.random.permutation(jax.random.fold_in(own, 1), rows)]
    offset_by = jax.random.randint(jax.random.fold_in(own, 2), (rows, 1), 0, top)
    return jnp.take_along_axis(listing, (jnp.arange(top)[None, :] + offset_by) % top, axis=1)


def load_shares(count, total, bound, skew, full):
    portions = [(1 << 20) // math.isqrt(standing ** skew) + 1 for standing in range(1, count + 1)]
    largest = bound if full else min(bound, max(-(-total // count), total * portions[0] // sum(portions)))
    least = 1 if total - largest >= count - 1 else 0
    counts, spare = [largest] + [least] * (count - 1), total - largest - least * (count - 1)
    while spare > 0:
        candidates = [i for i in range(1, count) if counts[i] < largest] or [i for i in range(1, count) if counts[i] < bound]
        pool, remaining = sum([portions[i] for i in candidates]), spare
        for i in candidates:
            extra = min(bound - counts[i], max(1, remaining * portions[i] // pool), spare)
            counts[i] = counts[i] + extra
            spare = spare - extra
    return np.array(counts)


def centred(stream_key, shape, deviation, reach, split=(), kind=jnp.bfloat16):
    values = deviation * jax.random.normal(stream_key, shape, jnp.float32)
    if split:
        values = values * block_scale(stream_key, shape, split, -0.22, 0.18)
    return jnp.clip(values, -reach, reach).astype(kind)


def setup_inputs(seed: int = 0) -> dict:
    key_list = jax.random.split(jax.random.key(seed), 6)
    hidden = centred(key_list[0], (WINDOW, SLOTS, FF), 1.0, 6.0, ((0, 4), (2, 8)))
    down_weight = centred(key_list[1], (WINDOW, FF, D), FF ** -0.5, 0.0625, ((0, 4), (1, 8)))
    expert_ids_keys = jax.random.split(jax.random.fold_in(key_list[2], 1), TOKENS // T_DP)
    expert_ids_turns = jax.random.permutation(jax.random.fold_in(key_list[2], 3), TOKENS // T_DP)
    expert_ids = jax.vmap(lambda own, number: assign_block(jax.random.fold_in(key_list[2], 2), own, number, T_DP, EXPERTS, 2, CAP, 2))(expert_ids_keys, expert_ids_turns).reshape((TOKENS, 2))
    combine = jnp.clip(0.1 + 0.9 * jax.random.uniform(key_list[3], (TOKENS, 2), jnp.float32) ** block_scale(key_list[3], (TOKENS, 2), ((0, 4),), -0.2, 0.2), 0.1, 1.0)
    out_grad = centred(key_list[4], (TOKENS, D), 1.0, 6.0, ((0, 4), (1, 8)))
    return dict(hidden=hidden, down_weight=down_weight, expert_ids=expert_ids, combine=combine, out_grad=out_grad)


def reference(hidden, down_weight, expert_ids, combine, out_grad):
    pair_ids = expert_ids.reshape(N_DP, 2 * T_DP).astype(jnp.int32)
    labels = jnp.arange(WINDOW, dtype=jnp.int32)
    onehot = (pair_ids[:, :, None] == labels[None, None, :]).astype(jnp.int32)
    pair_rank = jnp.sum((jnp.cumsum(onehot, axis=1) - 1) * onehot, axis=2)
    block_base = jnp.arange(N_DP, dtype=jnp.int32)[:, None] * CAP
    slot_index = (block_base + pair_rank).reshape(-1).astype(jnp.int32)
    flat_ids = pair_ids.reshape(-1)
    inside = flat_ids < WINDOW
    weights = combine.reshape(-1)
    repeated = jnp.repeat(out_grad, 2, axis=0).astype(jnp.float32)
    pair_grad = (weights[:, None] * repeated).astype(jnp.bfloat16)

    def per_expert(expert_items):
        expert_index, hidden_rows, weight = expert_items
        target = jnp.where(flat_ids == expert_index, slot_index, SLOTS).astype(jnp.int32)
        grad_rows = jnp.zeros((SLOTS, D), jnp.bfloat16).at[target].set(pair_grad, mode="drop")
        hid_grad = jnp.dot(grad_rows, weight.T, preferred_element_type=jnp.float32).astype(jnp.bfloat16)
        down_grad = jnp.dot(hidden_rows.T, grad_rows, preferred_element_type=jnp.float32).astype(jnp.bfloat16)
        out_rows = jnp.dot(hidden_rows, weight, preferred_element_type=jnp.float32).astype(jnp.bfloat16)
        return out_rows, hid_grad, down_grad

    out_rows, hidden_grad, weight_grad = lax.map(per_expert, (labels, hidden, down_weight))
    flat_rows = out_rows.reshape(WINDOW * SLOTS, D)
    pick_index = jnp.where(inside, flat_ids * SLOTS + slot_index, 0).astype(jnp.int32)
    picked = jnp.take(flat_rows, pick_index, axis=0).astype(jnp.float32)
    pair_coef = jnp.where(inside, weights, jnp.zeros_like(weights))
    mixed = jnp.sum((pair_coef[:, None] * picked).reshape(TOKENS, 2, D), axis=1).astype(jnp.bfloat16)
    return (mixed, hidden_grad, weight_grad)
```

```python
import functools

import jax
import jax.numpy as jnp
from jax import lax
from jax.experimental import pallas as pl
from jax.experimental.pallas import tpu as pltpu
from jax.sharding import PartitionSpec as P

BF, F32 = jnp.bfloat16, jnp.float32


def routed(hidden, down_weight, expert_ids, combine, out_grad):
    dp_count = lax.axis_size("dp")
    tok_rows = expert_ids.shape[0]
    capacity = 2 * tok_rows // dp_count
    slot_count = dp_count * capacity
    feat_share = out_grad.shape[1]
    width = down_weight.shape[2]
    flat_ids = expert_ids.reshape(-1)
    labels = jnp.arange(dp_count, dtype=jnp.int32)
    onehot = (flat_ids[:, None] == labels[None, :]).astype(jnp.int32)
    pair_rank = jnp.sum((jnp.cumsum(onehot, axis=0) - 1) * onehot, axis=1)
    inside = flat_ids < dp_count
    target = jnp.where(inside, flat_ids * capacity + pair_rank, dp_count * capacity)
    weights = combine.reshape(-1)
    full_grad = lax.all_gather(out_grad, "cuts", axis=1, tiled=True)
    scaled = (weights[:, None] * jnp.repeat(full_grad, 2, axis=0).astype(F32)).astype(BF)
    outgoing = jnp.zeros((dp_count * capacity, width), BF).at[target].set(scaled, mode="drop")
    incoming = lax.all_to_all(
        outgoing.reshape(dp_count, capacity, width), "dp", split_axis=0, concat_axis=0, tiled=True
    )
    grad_rows = incoming.reshape(slot_count, width)
    hidden_rows = hidden[0]
    weight = down_weight[0]
    own_share = lax.psum_scatter(
        lax.dot_general(weight, hidden_rows, (((0,), (1,)), ((), ())), preferred_element_type=F32),
        "cuts",
        scatter_dimension=0,
        tiled=True,
    )
    hid_grad = lax.dot_general(
        grad_rows, weight, (((1,), (1,)), ((), ())), preferred_element_type=F32
    ).astype(BF)
    down_grad = lax.dot_general(
        hidden_rows, grad_rows, (((0,), (0,)), ((), ())), preferred_element_type=F32
    ).astype(BF)
    returned = lax.all_to_all(
        own_share.astype(BF), "dp", split_axis=1, concat_axis=1, tiled=True
    )
    pick_index = jnp.minimum(target, dp_count * capacity - 1)
    picked = jnp.take(returned, pick_index, axis=1).astype(F32)
    pair_coef = jnp.where(inside, weights, jnp.zeros_like(weights))
    summed = jnp.sum((picked * pair_coef[None, :]).reshape(feat_share, tok_rows, 2), axis=2)
    mixed = summed.T.astype(BF)
    return (mixed, hid_grad[None], down_grad[None])


def routing(meta, expert, capacity):
    tok = meta.shape[1]
    label = jnp.full((1, tok), expert).astype(F32)
    first, second = meta[0:1] == label, meta[1:2] == label
    named = jnp.where(first, 1.0, jnp.where(second, 1.0, 0.0))
    weight = jnp.where(first, meta[2:3], jnp.where(second, meta[3:4], 0.0))
    earlier = lax.broadcasted_iota(jnp.int32, (tok, tok), 0) < lax.broadcasted_iota(
        jnp.int32, (tok, tok), 1
    )
    rank = jnp.dot(
        jnp.broadcast_to(named, (8, tok)).astype(BF),
        jnp.where(earlier, 1.0, 0.0).astype(BF),
        preferred_element_type=F32,
    )[0:1]
    slot = lax.broadcasted_iota(jnp.int32, (capacity, tok), 0).astype(F32)
    hot = jnp.where(slot == rank, named, 0.0)
    return hot, weight


def forward_kernel(capacity, hidden_ref, weight_ref, keep_ref, send_ref, rows_ref):
    me = lax.axis_index("dp")
    rows_ref[...] = jnp.dot(hidden_ref[0], weight_ref[0], preferred_element_type=F32)
    for dy in range(2):
        for dc, out in ((0, keep_ref), (1, send_ref)):
            source = me ^ (2 * dy + dc)
            at = pl.multiple_of(source * capacity, capacity)
            out[0, dy] = rows_ref[pl.ds(at, capacity), :].astype(BF)


def forward(hidden, weight, feat, dp_count):
    _, slots, ff = hidden.shape
    width = weight.shape[2]
    chunks, capacity = width // feat, slots // dp_count
    part = jax.ShapeDtypeStruct((chunks, 2, capacity, feat), BF)
    spec = pl.BlockSpec((1, 2, capacity, feat), lambda c: (c, 0, 0, 0))
    return pl.pallas_call(
        functools.partial(forward_kernel, capacity),
        grid=(chunks,),
        in_specs=[
            pl.BlockSpec((1, slots, ff), lambda c: (0, 0, 0)),
            pl.BlockSpec((1, ff, feat), lambda c: (0, 0, c)),
        ],
        out_specs=[spec, spec],
        out_shape=[part, part],
        scratch_shapes=[pltpu.VMEM((slots, feat), F32)],
        compiler_params=pltpu.CompilerParams(vmem_limit_bytes=24 << 20),
        cost_estimate=pl.CostEstimate(
            flops=2 * slots * ff * width, bytes_accessed=2 * (ff * width + slots * (ff + width)), transcendentals=0
        ),
        name="forward_rows",
    )(hidden, weight)


def spread_kernel(capacity, own_ref, near_ref, keep_ref, got_ref, *refs):
    outs, hots, cols = refs[:4], refs[4], refs[5]
    me, x = lax.axis_index("dp"), lax.axis_index("cuts") % 2

    @pl.when(pl.program_id(0) == 0)
    def _():
        for dy, meta_ref in enumerate((own_ref, near_ref)):
            for dc in range(2):
                hot, weight = routing(meta_ref[...], me ^ dc, capacity)
                tok = hot.shape[1]
                hots[dy, dc] = hot.astype(BF)
                cols[dy, dc] = jnp.broadcast_to(weight, (tok, tok)).T

    for dy in range(2):
        for dx in range(2):
            total = None
            for dc, rows in ((0, keep_ref), (1, got_ref)):
                picked = lax.dot_general(
                    hots[dy, dc], rows[0, x ^ dx, dy], (((0,), (0,)), ((), ())), preferred_element_type=F32
                )
                term = picked * cols[dy, dc][:, 0:1]
                total = term if total is None else total + term
            outs[2 * dy + dx][0] = total.astype(BF)


def spread(own, near, keep, got, nz):
    chunks, _, capacity, feat = keep.shape
    tok = own.shape[1]
    keep, got = (a.reshape(nz, 2, 2, capacity, feat) for a in (keep, got))
    rows = pl.BlockSpec((1, 2, 2, capacity, feat), lambda k: (k, 0, 0, 0, 0))
    meta = pl.BlockSpec((8, tok), lambda k: (0, 0))
    return pl.pallas_call(
        functools.partial(spread_kernel, capacity),
        grid=(nz,),
        in_specs=[meta, meta, rows, rows],
        out_specs=[pl.BlockSpec((1, tok, feat), lambda k: (k, 0, 0))] * 4,
        out_shape=[jax.ShapeDtypeStruct((nz, tok, feat), BF)] * 4,
        scratch_shapes=[pltpu.VMEM((2, 2, capacity, tok), BF), pltpu.VMEM((2, 2, tok, tok), F32)],
        compiler_params=pltpu.CompilerParams(vmem_limit_bytes=16 << 20),
        cost_estimate=pl.CostEstimate(
            flops=16 * tok * capacity * chunks * feat, bytes_accessed=24 * tok * chunks * feat, transcendentals=0
        ),
        name="spread_rows",
    )(own, near, keep, got)


def plane_sum_kernel(nz, a_ref, b_ref, c_ref, d_ref, *outs):
    z = lax.axis_index("cuts") // 2
    for k in range(nz):
        at = lax.rem(z + k, nz)
        total = (a_ref[at].astype(F32) + b_ref[at].astype(F32)) + (c_ref[at].astype(F32) + d_ref[at].astype(F32))
        outs[k][...] = total.astype(outs[k].dtype)


def plane_sum(parts):
    nz, tok, feat = parts[0].shape
    return pl.pallas_call(
        functools.partial(plane_sum_kernel, nz),
        out_shape=[jax.ShapeDtypeStruct((tok, feat), F32 if k == 0 else BF) for k in range(nz)],
        compiler_params=pltpu.CompilerParams(vmem_limit_bytes=16 << 20),
        name="plane_sum",
    )(*parts)


def backward_kernel(nz, capacity, pos_ref, hidden_ref, weight_ref, *refs):
    metas, grads, (hid_ref, down_ref), (hots, cols, turned, rows_ref, total) = (
        refs[:4], refs[4:12], refs[12:14], refs[14:],
    )
    step, me = pl.program_id(0), pos_ref[0]

    @pl.when(step == 0)
    def _():
        turned[...] = hidden_ref[0].T
        for q in range(4):
            hot, weight = routing(metas[q][...], me, capacity)
            hots[q] = hot.astype(BF)
            cols[q] = jnp.broadcast_to(jnp.sum(hot * weight, axis=1, keepdims=True), cols.shape[1:])

    def rows_of(dx):
        for q in range(4):
            picked = jnp.dot(hots[q], grads[4 * dx + q][0], preferred_element_type=F32)
            at = pl.multiple_of((me ^ q) * capacity, capacity)
            rows_ref[pl.ds(at, capacity), :] = (picked * cols[q][:, 0:1]).astype(BF)

    @pl.when(step < nz)
    def _():
        rows_of(0)

    @pl.when(step >= nz)
    def _():
        rows_of(1)

    rows = rows_ref[...]
    down_ref[0] = jnp.dot(turned[...], rows, preferred_element_type=F32).astype(BF)
    part = lax.dot_general(rows, weight_ref[0], (((1,), (1,)), ((), ())), preferred_element_type=F32)

    @pl.when(step == 0)
    def _():
        total[...] = part

    @pl.when(step > 0)
    def _():
        total[...] += part

    @pl.when(step == 2 * nz - 1)
    def _():
        hid_ref[0] = total[...].astype(BF)


def backward(pos, hidden, weight, metas, grads):
    nz, tok, feat = grads[0].shape
    _, slots, ff = hidden.shape
    width = weight.shape[2]
    capacity = slots // 4

    def column(g, pos):
        z = lax.rem(pos[2] - lax.rem(g, nz) + nz, nz)
        return (0, 0, 2 * z + (pos[1] ^ (g // nz)))

    first = pl.BlockSpec((1, tok, feat), lambda g, pos: (jnp.minimum(g, nz - 1), 0, 0))
    second = pl.BlockSpec((1, tok, feat), lambda g, pos: (jnp.maximum(g - nz, 0), 0, 0))
    whole = pl.BlockSpec((1, slots, ff), lambda g, pos: (0, 0, 0))
    return pl.pallas_call(
        functools.partial(backward_kernel, nz, capacity),
        grid_spec=pltpu.PrefetchScalarGridSpec(
            num_scalar_prefetch=1,
            grid=(2 * nz,),
            in_specs=[whole, pl.BlockSpec((1, ff, feat), column)]
            + [pl.BlockSpec((8, tok), lambda g, pos: (0, 0))] * 4
            + [first] * 4
            + [second] * 4,
            out_specs=[whole, pl.BlockSpec((1, ff, feat), column)],
            scratch_shapes=[
                pltpu.VMEM((4, capacity, tok), BF),
                pltpu.VMEM((4, capacity, 128), F32),
                pltpu.VMEM((ff, slots), BF),
                pltpu.VMEM((slots, feat), BF),
                pltpu.VMEM((slots, ff), F32),
            ],
        ),
        out_shape=[jax.ShapeDtypeStruct(hidden.shape, BF), jax.ShapeDtypeStruct(weight.shape, BF)],
        compiler_params=pltpu.CompilerParams(vmem_limit_bytes=32 << 20),
        cost_estimate=pl.CostEstimate(
            flops=4 * slots * ff * width,
            bytes_accessed=4 * ff * width + 4 * slots * ff + 8 * tok * width,
            transcendentals=0,
        ),
        name="backward_rows",
    )(pos, hidden, weight, *metas, *grads)


def shared(hidden, down_weight, expert_ids, combine, out_grad):
    dp_count, cut_count = lax.axis_size("dp"), lax.axis_size("cuts")
    nz = cut_count // 2
    tok, feat = out_grad.shape

    def send(value, dp_flip, cut_flip):
        pairs = [
            (d * cut_count + c, (d ^ dp_flip) * cut_count + (c ^ cut_flip))
            for d in range(dp_count)
            for c in range(cut_count)
        ]
        return lax.ppermute(value, ("dp", "cuts"), pairs)

    def along(value, k):
        return lax.ppermute(value, "cuts", [(c, (c + 2 * k) % cut_count) for c in range(cut_count)])

    pos = jnp.stack([lax.axis_index("dp"), lax.axis_index("cuts") % 2, lax.axis_index("cuts") // 2]).astype(jnp.int32)
    own = jnp.concatenate([expert_ids.T.astype(F32), combine.T, jnp.zeros((4, tok), F32)])
    near = send(own, 2, 0)
    blocks = jnp.stack([out_grad] + [along(out_grad, k) for k in range(1, nz)])

    keep, away = forward(hidden, down_weight, feat, dp_count)
    got = send(away, 1, 0)
    mine, by_x, by_y, by_xy = spread(own, near, keep, got, nz)
    by_xy, by_x, by_y = send(by_xy, 2, 1), send(by_x, 0, 1), send(by_y, 2, 0)

    metas = (own, send(own, 1, 0), near, send(near, 1, 0))
    grads = []
    for dx in range(2):
        for dy in range(2):
            part = blocks if dx == dy == 0 else send(blocks, 2 * dy, dx)
            grads += [part, send(part, 1, 0)]

    terms = plane_sum((mine, by_x, by_y, by_xy))
    total = terms[0]
    for k in range(1, nz):
        total = total + along(terms[k], k).astype(F32)
    mixed = total.astype(BF)

    hid_grad, down_grad = backward(pos, hidden, down_weight, metas, grads)
    return (mixed, hid_grad, down_grad)


def local(hidden, down_weight, expert_ids, combine, out_grad):
    dp_count, cut_count = lax.axis_size("dp"), lax.axis_size("cuts")
    few = dp_count == 4 and cut_count % 2 == 0 and dp_count * expert_ids.shape[0] <= 2 * hidden.shape[1]
    return (shared if few else routed)(hidden, down_weight, expert_ids, combine, out_grad)


def solution(mesh):
    return jax.shard_map(
        local,
        mesh=mesh,
        in_specs=(
            P("dp", None, "cuts"),
            P("dp", "cuts", None),
            P("dp", None),
            P("dp", None),
            P("dp", "cuts"),
        ),
        out_specs=(P("dp", "cuts"), P("dp", None, "cuts"), P("dp", "cuts", None)),
        check_vma=False,
    )
```

```python
import functools

import jax
import jax.numpy as jnp
from jax import lax
from jax.experimental import pallas as pl
from jax.experimental.pallas import tpu as pltpu
from jax.sharding import PartitionSpec as P

BF, F32 = jnp.bfloat16, jnp.float32


def routed(hidden, down_weight, expert_ids, combine, out_grad):
    dp_count = lax.axis_size("dp")
    tok_rows = expert_ids.shape[0]
    capacity = 2 * tok_rows // dp_count
    slot_count = dp_count * capacity
    feat_share = out_grad.shape[1]
    width = down_weight.shape[2]
    flat_ids = expert_ids.reshape(-1)
    labels = jnp.arange(dp_count, dtype=jnp.int32)
    onehot = (flat_ids[:, None] == labels[None, :]).astype(jnp.int32)
    pair_rank = jnp.sum((jnp.cumsum(onehot, axis=0) - 1) * onehot, axis=1)
    inside = flat_ids < dp_count
    target = jnp.where(inside, flat_ids * capacity + pair_rank, dp_count * capacity)
    weights = combine.reshape(-1)
    full_grad = lax.all_gather(out_grad, "cuts", axis=1, tiled=True)
    scaled = (weights[:, None] * jnp.repeat(full_grad, 2, axis=0).astype(F32)).astype(BF)
    outgoing = jnp.zeros((dp_count * capacity, width), BF).at[target].set(scaled, mode="drop")
    incoming = lax.all_to_all(
        outgoing.reshape(dp_count, capacity, width), "dp", split_axis=0, concat_axis=0, tiled=True
    )
    grad_rows = incoming.reshape(slot_count, width)
    hidden_rows = hidden[0]
    weight = down_weight[0]
    own_share = lax.psum_scatter(
        lax.dot_general(weight, hidden_rows, (((0,), (1,)), ((), ())), preferred_element_type=F32),
        "cuts",
        scatter_dimension=0,
        tiled=True,
    )
    hid_grad = lax.dot_general(
        grad_rows, weight, (((1,), (1,)), ((), ())), preferred_element_type=F32
    ).astype(BF)
    down_grad = lax.dot_general(
        hidden_rows, grad_rows, (((0,), (0,)), ((), ())), preferred_element_type=F32
    ).astype(BF)
    returned = lax.all_to_all(
        own_share.astype(BF), "dp", split_axis=1, concat_axis=1, tiled=True
    )
    pick_index = jnp.minimum(target, dp_count * capacity - 1)
    picked = jnp.take(returned, pick_index, axis=1).astype(F32)
    pair_coef = jnp.where(inside, weights, jnp.zeros_like(weights))
    summed = jnp.sum((picked * pair_coef[None, :]).reshape(feat_share, tok_rows, 2), axis=2)
    mixed = summed.T.astype(BF)
    return (mixed, hid_grad[None], down_grad[None])


def routing(meta, expert, capacity):
    tok = meta.shape[1]
    label = jnp.full((1, tok), expert).astype(F32)
    first, second = meta[0:1] == label, meta[1:2] == label
    named = jnp.where(first, 1.0, jnp.where(second, 1.0, 0.0))
    weight = jnp.where(first, meta[2:3], jnp.where(second, meta[3:4], 0.0))
    earlier = lax.broadcasted_iota(jnp.int32, (tok, tok), 0) < lax.broadcasted_iota(
        jnp.int32, (tok, tok), 1
    )
    rank = jnp.dot(
        jnp.broadcast_to(named, (8, tok)).astype(BF),
        jnp.where(earlier, 1.0, 0.0).astype(BF),
        preferred_element_type=F32,
    )[0:1]
    slot = lax.broadcasted_iota(jnp.int32, (capacity, tok), 0).astype(F32)
    hot = jnp.where(slot == rank, named, 0.0)
    return hot, weight


def forward_kernel(nz, capacity, ids_ref, coef_ref, hidden_ref, weight_ref, keep_ref, send_ref, meta_ref, *scratch):
    ids, held, wide, rows_ref, sems = scratch
    me = lax.axis_index("dp")
    feat = keep_ref.shape[-1]
    copies = [pltpu.make_async_copy(hidden_ref.at[0], held, sems.at[nz])]
    for z in range(nz):
        part = weight_ref.at[0, :, pl.ds(2 * z * feat, 2 * feat)]
        copies.append(pltpu.make_async_copy(part, wide.at[z], sems.at[z]))
    small = pltpu.make_async_copy(ids_ref, ids, sems.at[nz + 1])
    small.start()
    coefs = pltpu.make_async_copy(coef_ref, meta_ref.at[2:4], sems.at[nz + 2])
    coefs.start()
    for copy in copies:
        copy.start()
    small.wait()
    meta_ref[0:2] = ids[...].astype(F32)
    coefs.wait()
    copies[0].wait()
    for z in range(nz):
        copies[z + 1].wait()
        rows_ref[...] = jnp.dot(held[...], wide[z], preferred_element_type=F32).astype(BF)
        for dy in range(2):
            for dc, out in ((0, keep_ref), (1, send_ref)):
                source = me ^ (2 * dy + dc)
                at = pl.multiple_of(source * capacity, capacity)
                for x in range(2):
                    out[z, x, dy] = rows_ref[pl.ds(at, capacity), x * feat : (x + 1) * feat]


def forward(ids, coefs, hidden, weight, feat, dp_count):
    _, slots, ff = hidden.shape
    width = weight.shape[2]
    nz, capacity = width // (2 * feat), slots // dp_count
    part = jax.ShapeDtypeStruct((nz, 2, 2, capacity, feat), BF)
    hbm, vmem = pl.BlockSpec(memory_space=pltpu.HBM), pl.BlockSpec(memory_space=pltpu.VMEM)
    return pl.pallas_call(
        functools.partial(forward_kernel, nz, capacity),
        in_specs=[hbm] * 4,
        out_specs=[vmem] * 3,
        out_shape=[part, part, jax.ShapeDtypeStruct((4, ids.shape[1]), F32)],
        scratch_shapes=[
            pltpu.VMEM(ids.shape, jnp.int32),
            pltpu.VMEM((slots, ff), BF),
            pltpu.VMEM((nz, ff, 2 * feat), BF),
            pltpu.VMEM((slots, 2 * feat), BF),
            pltpu.SemaphoreType.DMA((nz + 3,)),
        ],
        compiler_params=pltpu.CompilerParams(vmem_limit_bytes=58 << 20),
        cost_estimate=pl.CostEstimate(
            flops=2 * slots * ff * width, bytes_accessed=2 * (ff * width + slots * (ff + width)), transcendentals=0
        ),
        name="forward_rows",
    )(ids, coefs, hidden, weight)


def spread_kernel(nz, capacity, own_ref, near_ref, keep_ref, got_ref, *refs):
    (to_x, by_x, to_y, by_y), hots, cols = refs[:4], refs[4], refs[5]
    step, me, x = pl.program_id(0), lax.axis_index("dp"), lax.axis_index("cuts") % 2

    @pl.when(step == 0)
    def _():
        for dy, meta_ref in enumerate((own_ref, near_ref)):
            for dc in range(2):
                hot, weight = routing(meta_ref[...], me ^ dc, capacity)
                tok = hot.shape[1]
                hots[dy, dc] = hot.astype(BF)
                cols[dy, dc] = jnp.broadcast_to(weight, (tok, tok)).T

    def block(dy, dx):
        total = None
        for dc, rows in ((0, keep_ref), (1, got_ref)):
            picked = lax.dot_general(
                hots[dy, dc], rows[0, x ^ dx, dy], (((0,), (0,)), ((), ())), preferred_element_type=F32
            )
            term = picked * cols[dy, dc][:, 0:1]
            total = term if total is None else total + term
        return total

    @pl.when(step < nz // 2)
    def _():
        for dy in range(2):
            to_x[dy, 0] = block(dy, 1).astype(BF)
            by_x[dy, 0] = block(dy, 0)

    @pl.when(step >= nz // 2)
    def _():
        for dx in range(2):
            to_y[dx, 0] = block(1, dx).astype(BF)
            by_y[dx, 0] = block(0, dx)


def spread(own, near, keep, got):
    nz, _, _, capacity, feat = keep.shape
    tok, half = own.shape[1], nz // 2
    rows = pl.BlockSpec((1, 2, 2, capacity, feat), lambda k: (k, 0, 0, 0, 0))
    meta = pl.BlockSpec((4, tok), lambda k: (0, 0))
    first = pl.BlockSpec((2, 1, tok, feat), lambda k: (0, jnp.minimum(k, half - 1), 0, 0))
    second = pl.BlockSpec((2, 1, tok, feat), lambda k: (0, jnp.maximum(k - half, 0), 0, 0))
    shape = (2, half, tok, feat)
    return pl.pallas_call(
        functools.partial(spread_kernel, nz, capacity),
        grid=(nz,),
        in_specs=[meta, meta, rows, rows],
        out_specs=[first, first, second, second],
        out_shape=[jax.ShapeDtypeStruct(shape, t) for t in (BF, F32, BF, F32)],
        scratch_shapes=[pltpu.VMEM((2, 2, capacity, tok), BF), pltpu.VMEM((2, 2, tok, tok), F32)],
        compiler_params=pltpu.CompilerParams(vmem_limit_bytes=16 << 20),
        cost_estimate=pl.CostEstimate(
            flops=32 * tok * capacity * nz * feat, bytes_accessed=48 * tok * nz * feat, transcendentals=0
        ),
        name="spread_rows",
    )(own, near, keep, got)


def first_sum_kernel(kept_ref, got_ref, keep_out, send_out):
    keep_out[...] = kept_ref[0] + got_ref[0].astype(F32)
    send_out[...] = (kept_ref[1] + got_ref[1].astype(F32)).astype(BF)


def first_sum(kept, got):
    shape = kept.shape[1:]
    return pl.pallas_call(
        first_sum_kernel,
        out_shape=[jax.ShapeDtypeStruct(shape, F32), jax.ShapeDtypeStruct(shape, BF)],
        compiler_params=pltpu.CompilerParams(vmem_limit_bytes=16 << 20),
        name="first_sum",
    )(kept, got)


def second_sum_kernel(nz, a_ref, a_got, b_ref, b_got, *refs):
    outs, total = refs[:nz], refs[nz]
    z, half = lax.axis_index("cuts") // 2, nz // 2
    total[:half] = a_ref[...] + a_got[...].astype(F32)
    total[half:] = b_ref[...] + b_got[...].astype(F32)
    for k in range(nz):
        outs[k][...] = total[lax.rem(z + k, nz)].astype(outs[k].dtype)


def second_sum(a, a_got, b, b_got):
    half, tok, feat = a.shape
    nz = 2 * half
    return pl.pallas_call(
        functools.partial(second_sum_kernel, nz),
        out_shape=[jax.ShapeDtypeStruct((tok, feat), F32 if k == 0 else BF) for k in range(nz)],
        scratch_shapes=[pltpu.VMEM((nz, tok, feat), F32)],
        compiler_params=pltpu.CompilerParams(vmem_limit_bytes=16 << 20),
        name="second_sum",
    )(a, a_got, b, b_got)


def stack_kernel(_, *refs):
    for k, ref in enumerate(refs[:-1]):
        refs[-1][k] = ref[...]


def stack(parts, after):
    vmem = pl.BlockSpec(memory_space=pltpu.VMEM)
    return pl.pallas_call(
        stack_kernel,
        in_specs=[pl.BlockSpec(memory_space=pl.ANY)] + [vmem] * len(parts),
        out_specs=vmem,
        out_shape=jax.ShapeDtypeStruct((len(parts), *parts[0].shape), parts[0].dtype),
        compiler_params=pltpu.CompilerParams(vmem_limit_bytes=16 << 20),
        name="stack_blocks",
    )(after, *parts)


def backward_kernel(nz, capacity, *refs):
    hidden_ref, weight_ref = refs[:2]
    metas, grads, (hid_out, down_out, mark) = refs[2:6], refs[6:16], refs[16:19]
    made, rows_ref, turned, total, done, hots, cols, sems = refs[19:]
    me, x, z = lax.axis_index("dp"), lax.axis_index("cuts") % 2, lax.axis_index("cuts") // 2
    feat, half = grads[0].shape[-1], nz // 2

    for q in range(4):
        hot, weight = routing(metas[q][...], me, capacity)
        hots[q] = hot.astype(BF)
        cols[q] = jnp.broadcast_to(jnp.sum(hot * weight, axis=1, keepdims=True), cols.shape[1:])
    turned[...] = hidden_ref[0].T

    def put(dx, q, rows):
        lane = pl.multiple_of((x ^ dx) * feat, feat)
        at = pl.multiple_of((me ^ q) * capacity, capacity)
        picked = jnp.dot(hots[q], rows, preferred_element_type=F32)
        rows_ref[pl.ds(at, capacity), pl.ds(lane, feat)] = (picked * cols[q][:, 0:1]).astype(BF)

    leaving = []
    for k in range(nz):
        for dc in range(2):
            own, by_x, by_y, low, high = grads[5 * dc : 5 * dc + 5]
            put(0, dc, own[k])
            put(1, dc, by_x[k])
            put(0, 2 + dc, by_y[k])
            put(1, 2 + dc, low[k] if k < half else high[k - half])
        rows = rows_ref[...]
        column = pl.ds(pl.multiple_of(lax.rem(z - k + nz, nz) * 2 * feat, 2 * feat), 2 * feat)
        part = lax.dot_general(rows, weight_ref[0, :, column], (((1,), (1,)), ((), ())), preferred_element_type=F32)
        total[...] = part if k == 0 else total[...] + part
        if k == nz - 1:
            done[...] = total[...].astype(BF)
            last = pltpu.make_async_copy(done, hid_out.at[0], sems.at[2])
            last.start()
        if k >= 2:
            leaving[k - 2].wait()
        made[k % 2] = jnp.dot(turned[...], rows, preferred_element_type=F32).astype(BF)
        leaving.append(pltpu.make_async_copy(made.at[k % 2], down_out.at[0, :, column], sems.at[k % 2]))
        leaving[k].start()
    for copy in leaving[-2:]:
        copy.wait()
    last.wait()
    mark[...] = jnp.zeros_like(mark)


def backward(hidden, weight, metas, grads):
    nz, tok, feat = grads[0].shape
    _, slots, ff = hidden.shape
    width = weight.shape[2]
    capacity = slots // 4
    anywhere, vmem = pl.BlockSpec(memory_space=pl.ANY), pl.BlockSpec(memory_space=pltpu.VMEM)
    return pl.pallas_call(
        functools.partial(backward_kernel, nz, capacity),
        in_specs=[vmem] * 16,
        out_specs=[anywhere, anywhere, vmem],
        scratch_shapes=[
            pltpu.VMEM((2, ff, 2 * feat), BF),
            pltpu.VMEM((slots, 2 * feat), BF),
            pltpu.VMEM((ff, slots), BF),
            pltpu.VMEM((slots, ff), F32),
            pltpu.VMEM((slots, ff), BF),
            pltpu.VMEM((4, capacity, tok), BF),
            pltpu.VMEM((4, capacity, 128), F32),
            pltpu.SemaphoreType.DMA((3,)),
        ],
        out_shape=[
            jax.ShapeDtypeStruct(hidden.shape, BF),
            jax.ShapeDtypeStruct(weight.shape, BF),
            jax.ShapeDtypeStruct((8, 128), F32),
        ],
        compiler_params=pltpu.CompilerParams(vmem_limit_bytes=32 << 20),
        cost_estimate=pl.CostEstimate(
            flops=4 * slots * ff * width,
            bytes_accessed=4 * ff * width + 4 * slots * ff + 8 * tok * width,
            transcendentals=0,
        ),
        name="backward_rows",
    )(hidden, weight, *metas, *grads)


def last_sum_kernel(_, first_ref, *refs):
    total = first_ref[...]
    for ref in refs[:-1]:
        total = total + ref[...].astype(F32)
    refs[-1][...] = total.astype(BF)


def last_sum(parts, after):
    vmem = pl.BlockSpec(memory_space=pltpu.VMEM)
    return pl.pallas_call(
        last_sum_kernel,
        in_specs=[pl.BlockSpec(memory_space=pl.ANY)] + [vmem] * len(parts),
        out_specs=vmem,
        out_shape=jax.ShapeDtypeStruct(parts[0].shape, BF),
        compiler_params=pltpu.CompilerParams(vmem_limit_bytes=16 << 20),
        name="last_sum",
    )(after, *parts)


def shared(hidden, down_weight, expert_ids, combine, out_grad):
    dp_count, cut_count = lax.axis_size("dp"), lax.axis_size("cuts")
    nz = cut_count // 2
    tok, feat = out_grad.shape

    def send(value, dp_flip, cut_flip):
        pairs = [
            (d * cut_count + c, (d ^ dp_flip) * cut_count + (c ^ cut_flip))
            for d in range(dp_count)
            for c in range(cut_count)
        ]
        return lax.ppermute(value, ("dp", "cuts"), pairs)

    def along(value, k):
        return lax.ppermute(value, "cuts", [(c, (c + 2 * k) % cut_count) for c in range(cut_count)])

    half = nz // 2
    keep, away, own = forward(expert_ids.T, combine.T, hidden, down_weight, feat, dp_count)
    near = send(own, 2, 0)
    got = send(away, 1, 0)
    to_x, by_x, to_y, by_y = spread(own, near, keep, got)
    mine, _ = lax.optimization_barrier((out_grad, by_x))
    blocks = [mine] + [along(mine, k) for k in range(1, nz)]
    a, a_send = first_sum(by_x, send(to_x, 0, 1))
    b, b_send = first_sum(by_y, send(to_y, 2, 0))
    terms = second_sum(a, send(a_send, 2, 0), b, send(b_send, 0, 1))
    blocks = stack(blocks, a)
    from_x, from_y = send(blocks, 0, 1), send(blocks, 2, 0)
    parts = [blocks, from_x, from_y, send(from_x[:half], 2, 0), send(from_y[half:], 0, 1)]
    grads = parts + [send(p, 1, 0) for p in parts]
    metas = (own, send(own, 1, 0), near, send(near, 1, 0))
    hid_grad, down_grad, mark = backward(hidden, down_weight, metas, grads)
    mixed = last_sum([terms[0]] + [along(terms[k], k) for k in range(1, nz)], mark)
    return (mixed, hid_grad, down_grad)


def local(hidden, down_weight, expert_ids, combine, out_grad):
    dp_count, cut_count = lax.axis_size("dp"), lax.axis_size("cuts")
    few = dp_count == 4 and cut_count % 4 == 0 and dp_count * expert_ids.shape[0] <= 2 * hidden.shape[1]
    return (shared if few else routed)(hidden, down_weight, expert_ids, combine, out_grad)


def solution(mesh):
    return jax.shard_map(
        local,
        mesh=mesh,
        in_specs=(
            P("dp", None, "cuts"),
            P("dp", "cuts", None),
            P("dp", None),
            P("dp", None),
            P("dp", "cuts"),
        ),
        out_specs=(P("dp", "cuts"), P("dp", None, "cuts"), P("dp", "cuts", None)),
        check_vma=False,
    )
```

```python
import functools

import jax
import jax.numpy as jnp
from jax import lax
from jax.experimental import pallas as pl
from jax.experimental.pallas import tpu as pltpu
from jax.sharding import PartitionSpec as P

BF, F32 = jnp.bfloat16, jnp.float32


def routed(hidden, down_weight, expert_ids, combine, out_grad):
    dp_count = lax.axis_size("dp")
    tok_rows = expert_ids.shape[0]
    capacity = 2 * tok_rows // dp_count
    slot_count = dp_count * capacity
    feat_share = out_grad.shape[1]
    width = down_weight.shape[2]
    flat_ids = expert_ids.reshape(-1)
    labels = jnp.arange(dp_count, dtype=jnp.int32)
    onehot = (flat_ids[:, None] == labels[None, :]).astype(jnp.int32)
    pair_rank = jnp.sum((jnp.cumsum(onehot, axis=0) - 1) * onehot, axis=1)
    inside = flat_ids < dp_count
    target = jnp.where(inside, flat_ids * capacity + pair_rank, dp_count * capacity)
    weights = combine.reshape(-1)
    full_grad = lax.all_gather(out_grad, "cuts", axis=1, tiled=True)
    scaled = (weights[:, None] * jnp.repeat(full_grad, 2, axis=0).astype(F32)).astype(BF)
    outgoing = jnp.zeros((dp_count * capacity, width), BF).at[target].set(scaled, mode="drop")
    incoming = lax.all_to_all(
        outgoing.reshape(dp_count, capacity, width), "dp", split_axis=0, concat_axis=0, tiled=True
    )
    grad_rows = incoming.reshape(slot_count, width)
    hidden_rows = hidden[0]
    weight = down_weight[0]
    own_share = lax.psum_scatter(
        lax.dot_general(weight, hidden_rows, (((0,), (1,)), ((), ())), preferred_element_type=F32),
        "cuts",
        scatter_dimension=0,
        tiled=True,
    )
    hid_grad = lax.dot_general(
        grad_rows, weight, (((1,), (1,)), ((), ())), preferred_element_type=F32
    ).astype(BF)
    down_grad = lax.dot_general(
        hidden_rows, grad_rows, (((0,), (0,)), ((), ())), preferred_element_type=F32
    ).astype(BF)
    returned = lax.all_to_all(
        own_share.astype(BF), "dp", split_axis=1, concat_axis=1, tiled=True
    )
    pick_index = jnp.minimum(target, dp_count * capacity - 1)
    picked = jnp.take(returned, pick_index, axis=1).astype(F32)
    pair_coef = jnp.where(inside, weights, jnp.zeros_like(weights))
    summed = jnp.sum((picked * pair_coef[None, :]).reshape(feat_share, tok_rows, 2), axis=2)
    mixed = summed.T.astype(BF)
    return (mixed, hid_grad[None], down_grad[None])


def routing(meta, expert, capacity):
    tok = meta.shape[1]
    label = jnp.full((1, tok), expert).astype(F32)
    first, second = meta[0:1] == label, meta[1:2] == label
    named = jnp.where(first, 1.0, jnp.where(second, 1.0, 0.0))
    weight = jnp.where(first, meta[2:3], jnp.where(second, meta[3:4], 0.0))
    earlier = lax.broadcasted_iota(jnp.int32, (tok, tok), 0) < lax.broadcasted_iota(
        jnp.int32, (tok, tok), 1
    )
    rank = jnp.dot(
        jnp.broadcast_to(named, (8, tok)).astype(BF),
        jnp.where(earlier, 1.0, 0.0).astype(BF),
        preferred_element_type=F32,
    )[0:1]
    slot = lax.broadcasted_iota(jnp.int32, (capacity, tok), 0).astype(F32)
    hot = jnp.where(slot == rank, named, 0.0)
    return hot, weight


def forward_kernel(nz, capacity, ids_ref, coef_ref, hidden_ref, weight_ref, keep_ref, send_ref, meta_ref, *scratch):
    ids, held, wide, part, rows, sems = scratch
    me = lax.axis_index("dp")
    feat = keep_ref.shape[-1]
    ff = wide.shape[0]
    mid = ff // 2
    small = pltpu.make_async_copy(ids_ref, ids, sems.at[0])
    coefs = pltpu.make_async_copy(coef_ref, meta_ref.at[2:4], sems.at[1])
    first = pltpu.make_async_copy(hidden_ref.at[0], held, sems.at[2])
    low = pltpu.make_async_copy(weight_ref.at[0, pl.ds(0, mid)], wide.at[pl.ds(0, mid)], sems.at[3])
    high = pltpu.make_async_copy(weight_ref.at[0, pl.ds(mid, mid)], wide.at[pl.ds(mid, mid)], sems.at[4])
    for copy in (small, coefs, first, low, high):
        copy.start()
    small.wait()
    meta_ref[0:2] = ids[...].astype(F32)
    coefs.wait()
    first.wait()
    low.wait()
    for z in range(nz):
        columns = slice(2 * z * feat, 2 * (z + 1) * feat)
        part[z] = jnp.dot(held[:, :mid], wide[:mid, columns], preferred_element_type=F32)
    high.wait()
    for z in range(nz):
        columns = slice(2 * z * feat, 2 * (z + 1) * feat)
        rest = jnp.dot(held[:, mid:], wide[mid:, columns], preferred_element_type=F32)
        rows[...] = (part[z] + rest).astype(BF)
        for dy in range(2):
            for dc, out in ((0, keep_ref), (1, send_ref)):
                at = pl.multiple_of((me ^ (2 * dy + dc)) * capacity, capacity)
                for x in range(2):
                    out[z, x, dy] = rows[pl.ds(at, capacity), x * feat : (x + 1) * feat]


def forward(ids, coefs, hidden, weight, feat, dp_count):
    _, slots, ff = hidden.shape
    width = weight.shape[2]
    nz, capacity = width // (2 * feat), slots // dp_count
    part = jax.ShapeDtypeStruct((nz, 2, 2, capacity, feat), BF)
    hbm, vmem = pl.BlockSpec(memory_space=pltpu.HBM), pl.BlockSpec(memory_space=pltpu.VMEM)
    return pl.pallas_call(
        functools.partial(forward_kernel, nz, capacity),
        in_specs=[hbm] * 4,
        out_specs=[vmem] * 3,
        out_shape=[part, part, jax.ShapeDtypeStruct((4, ids.shape[1]), F32)],
        scratch_shapes=[
            pltpu.VMEM(ids.shape, jnp.int32),
            pltpu.VMEM((slots, ff), BF),
            pltpu.VMEM((ff, width), BF),
            pltpu.VMEM((nz, slots, 2 * feat), F32),
            pltpu.VMEM((slots, 2 * feat), BF),
            pltpu.SemaphoreType.DMA((5,)),
        ],
        compiler_params=pltpu.CompilerParams(vmem_limit_bytes=50 << 20),
        cost_estimate=pl.CostEstimate(
            flops=2 * slots * ff * width, bytes_accessed=2 * (ff * width + slots * (ff + width)), transcendentals=0
        ),
        name="forward_rows",
    )(ids, coefs, hidden, weight)


def spread_kernel(nz, capacity, own_ref, near_ref, keep_ref, got_ref, grad_ref, *refs):
    to_x, by_x, to_y, by_y = refs
    me, x = lax.axis_index("dp"), lax.axis_index("cuts") % 2
    tok = grad_ref.shape[0]
    half = nz // 2
    to_x[nz] = grad_ref[...]
    to_y[nz] = grad_ref[...]
    for dy, meta_ref in enumerate((own_ref, near_ref)):
        hots, cols = [], []
        for dc in range(2):
            hot, weight = routing(meta_ref[...], me ^ dc, capacity)
            hots.append(hot.astype(BF))
            cols.append(jnp.broadcast_to(weight, (tok, tok)).T[:, 0:1])

        def block(z, dx):
            total = None
            for dc, rows in ((0, keep_ref), (1, got_ref)):
                picked = lax.dot_general(
                    hots[dc], rows[z, x ^ dx, dy], (((0,), (0,)), ((), ())), preferred_element_type=F32
                )
                term = picked * cols[dc]
                total = term if total is None else total + term
            return total

        for z in range(half):
            to_x[half * dy + z] = block(z, 1).astype(BF)
            by_x[half * dy + z] = block(z, 0)
            for dx in range(2):
                if dy:
                    to_y[half * dx + z] = block(half + z, dx).astype(BF)
                else:
                    by_y[half * dx + z] = block(half + z, dx)


def spread(own, near, keep, got, grad):
    nz, _, _, capacity, _ = keep.shape
    tok, feat = grad.shape
    shapes = [jax.ShapeDtypeStruct((nz + 1, tok, feat), BF), jax.ShapeDtypeStruct((nz, tok, feat), F32)] * 2
    return pl.pallas_call(
        functools.partial(spread_kernel, nz, capacity),
        out_shape=shapes,
        compiler_params=pltpu.CompilerParams(vmem_limit_bytes=24 << 20),
        cost_estimate=pl.CostEstimate(
            flops=32 * tok * capacity * nz * feat, bytes_accessed=48 * tok * nz * feat, transcendentals=0
        ),
        name="spread_rows",
    )(own, near, keep, got, grad)


def first_sum_kernel(half, _, x_kept, x_got, y_kept, y_got, *refs):
    far, (x_keep, x_send, y_keep, y_send, own, stacked) = refs[:-6], refs[-6:]
    for k, ref in enumerate(far):
        stacked[k] = ref[...]
    own[0] = x_got[2 * half]
    own[1] = y_got[2 * half]
    for kept, got, keep, send in ((x_kept, x_got, x_keep, x_send), (y_kept, y_got, y_keep, y_send)):
        for z in range(half):
            keep[z] = kept[z] + got[z].astype(F32)
            send[z] = (kept[half + z] + got[half + z].astype(F32)).astype(BF)


def first_sum(after, x_kept, x_got, y_kept, y_got, far):
    nz, tok, feat = x_kept.shape
    half = nz // 2
    shapes = [
        jax.ShapeDtypeStruct((half, tok, feat), F32),
        jax.ShapeDtypeStruct((half, tok, feat), BF),
    ]
    return pl.pallas_call(
        functools.partial(first_sum_kernel, half),
        in_specs=[pl.BlockSpec(memory_space=pl.ANY)] + [pl.BlockSpec(memory_space=pltpu.VMEM)] * (4 + len(far)),
        out_shape=shapes + shapes + [jax.ShapeDtypeStruct((n, tok, feat), BF) for n in (2, len(far))],
        compiler_params=pltpu.CompilerParams(vmem_limit_bytes=16 << 20),
        cost_estimate=pl.CostEstimate(flops=1000_000_000, bytes_accessed=0, transcendentals=0),
        name="first_sum",
    )(after, x_kept, x_got, y_kept, y_got, *far)


def second_sum_kernel(nz, x_kept, y_kept, by_y, by_x, *refs):
    outs, total = refs[:nz], refs[nz]
    z, half = lax.axis_index("cuts") // 2, nz // 2
    total[:half] = x_kept[...] + by_y[...].astype(F32)
    total[half:] = y_kept[...] + by_x[...].astype(F32)
    for k in range(nz):
        outs[k][...] = total[lax.rem(z + k, nz)].astype(outs[k].dtype)


def second_sum(x_kept, y_kept, by_y, by_x):
    half, tok, feat = x_kept.shape
    nz = 2 * half
    return pl.pallas_call(
        functools.partial(second_sum_kernel, nz),
        out_shape=[jax.ShapeDtypeStruct((tok, feat), F32 if k == 0 else BF) for k in range(nz)],
        scratch_shapes=[pltpu.VMEM((nz, tok, feat), F32)],
        compiler_params=pltpu.CompilerParams(vmem_limit_bytes=16 << 20),
        cost_estimate=pl.CostEstimate(flops=5000_000_000, bytes_accessed=0, transcendentals=0),
        name="second_sum",
    )(x_kept, y_kept, by_y, by_x)


def stack_kernel(_, *refs):
    for k, ref in enumerate(refs[:-1]):
        refs[-1][k] = ref[...]


def stack(parts, after):
    vmem = pl.BlockSpec(memory_space=pltpu.VMEM)
    return pl.pallas_call(
        stack_kernel,
        in_specs=[pl.BlockSpec(memory_space=pl.ANY)] + [vmem] * len(parts),
        out_specs=vmem,
        out_shape=jax.ShapeDtypeStruct((len(parts), *parts[0].shape), parts[0].dtype),
        compiler_params=pltpu.CompilerParams(vmem_limit_bytes=16 << 20),
        cost_estimate=pl.CostEstimate(flops=1000_000_000, bytes_accessed=0, transcendentals=0),
        name="stack_blocks",
    )(after, *parts)


PER_CORE = 7


def backward_kernel(nz, capacity, *refs):
    hidden_ref, weight_ref = refs[:2]
    metas, grads, refs = refs[2:6], refs[6 : 6 + 2 * PER_CORE], refs[-11:]
    hid_out, down_out, mark = refs[:3]
    made, rows_ref, turned, total, done, hots, cols, sems = refs[3:]
    me, x, z = lax.axis_index("dp"), lax.axis_index("cuts") % 2, lax.axis_index("cuts") // 2
    feat = grads[0].shape[-1]

    for q in range(4):
        hot, weight = routing(metas[q][...], me, capacity)
        hots[q] = hot.astype(BF)
        cols[q] = jnp.broadcast_to(jnp.sum(hot * weight, axis=1, keepdims=True), cols.shape[1:])
    turned[...] = hidden_ref[0].T

    def put(dx, q, rows):
        lane = pl.multiple_of((x ^ dx) * feat, feat)
        at = pl.multiple_of((me ^ q) * capacity, capacity)
        picked = jnp.dot(hots[q], rows, preferred_element_type=F32)
        rows_ref[pl.ds(at, capacity), pl.ds(lane, feat)] = (picked * cols[q][:, 0:1]).astype(BF)

    leaving = []
    for k in range(nz):
        for dc in range(2):
            own, cross, plane, far, far_x, far_y, far_xy = grads[PER_CORE * dc : PER_CORE * (dc + 1)]
            put(0, dc, own[...] if k == 0 else far[k - 1])
            put(1, dc, plane[0] if k == 0 else far_x[k - 1])
            put(0, 2 + dc, plane[1] if k == 0 else far_y[k - 1])
            put(1, 2 + dc, cross[...] if k == 0 else far_xy[k - 1])
        rows = rows_ref[...]
        column = pl.ds(pl.multiple_of(lax.rem(z - k + nz, nz) * 2 * feat, 2 * feat), 2 * feat)
        part = lax.dot_general(rows, weight_ref[0, :, column], (((1,), (1,)), ((), ())), preferred_element_type=F32)
        total[...] = part if k == 0 else total[...] + part
        if k == nz - 1:
            done[...] = total[...].astype(BF)
            last = pltpu.make_async_copy(done, hid_out.at[0], sems.at[2])
            last.start()
        if k >= 2:
            leaving[k - 2].wait()
        made[k % 2] = jnp.dot(turned[...], rows, preferred_element_type=F32).astype(BF)
        leaving.append(pltpu.make_async_copy(made.at[k % 2], down_out.at[0, :, column], sems.at[k % 2]))
        leaving[k].start()
    for copy in leaving[-2:]:
        copy.wait()
    last.wait()
    mark[...] = jnp.zeros_like(mark)


def backward(hidden, weight, metas, grads, after):
    tok, feat = grads[0].shape
    _, slots, ff = hidden.shape
    width = weight.shape[2]
    nz, capacity = width // (2 * feat), slots // 4
    anywhere, vmem = pl.BlockSpec(memory_space=pl.ANY), pl.BlockSpec(memory_space=pltpu.VMEM)
    return pl.pallas_call(
        functools.partial(backward_kernel, nz, capacity),
        in_specs=[vmem] * (6 + 2 * PER_CORE) + [anywhere] * len(after),
        out_specs=[anywhere, anywhere, vmem],
        scratch_shapes=[
            pltpu.VMEM((2, ff, 2 * feat), BF),
            pltpu.VMEM((slots, 2 * feat), BF),
            pltpu.VMEM((ff, slots), BF),
            pltpu.VMEM((slots, ff), F32),
            pltpu.VMEM((slots, ff), BF),
            pltpu.VMEM((4, capacity, tok), BF),
            pltpu.VMEM((4, capacity, 128), F32),
            pltpu.SemaphoreType.DMA((3,)),
        ],
        out_shape=[
            jax.ShapeDtypeStruct(hidden.shape, BF),
            jax.ShapeDtypeStruct(weight.shape, BF),
            jax.ShapeDtypeStruct((8, 128), F32),
        ],
        compiler_params=pltpu.CompilerParams(vmem_limit_bytes=32 << 20),
        cost_estimate=pl.CostEstimate(flops=3000_000_000, bytes_accessed=0, transcendentals=0),
        name="backward_rows",
    )(hidden, weight, *metas, *grads, *after)


def last_sum_kernel(_, first_ref, *refs):
    total = first_ref[...]
    for ref in refs[:-1]:
        total = total + ref[...].astype(F32)
    refs[-1][...] = total.astype(BF)


def last_sum(parts, after):
    vmem = pl.BlockSpec(memory_space=pltpu.VMEM)
    return pl.pallas_call(
        last_sum_kernel,
        in_specs=[pl.BlockSpec(memory_space=pl.ANY)] + [vmem] * len(parts),
        out_specs=vmem,
        out_shape=jax.ShapeDtypeStruct(parts[0].shape, BF),
        compiler_params=pltpu.CompilerParams(vmem_limit_bytes=16 << 20),
        cost_estimate=pl.CostEstimate(flops=1000_000_000, bytes_accessed=0, transcendentals=0),
        name="last_sum",
    )(after, *parts)


def shared(hidden, down_weight, expert_ids, combine, out_grad):
    dp_count, cut_count = lax.axis_size("dp"), lax.axis_size("cuts")
    nz = cut_count // 2
    feat = out_grad.shape[1]

    def send(value, dp_flip, cut_flip):
        pairs = [
            (d * cut_count + c, (d ^ dp_flip) * cut_count + (c ^ cut_flip))
            for d in range(dp_count)
            for c in range(cut_count)
        ]
        return lax.ppermute(value, ("dp", "cuts"), pairs)

    def along(value, k):
        return lax.ppermute(value, "cuts", [(c, (c + 2 * k) % cut_count) for c in range(cut_count)])

    keep, away, own = forward(expert_ids.T, combine.T, hidden, down_weight, out_grad.shape[1], dp_count)
    near = send(own, 2, 0)
    got = send(away, 1, 0)
    to_x, by_x, to_y, by_y = spread(own, near, keep, got, out_grad)
    mine, _ = lax.optimization_barrier((out_grad, by_x))
    far = [along(mine, k) for k in range(1, nz)]
    cross = send(mine, 2, 1)
    a, a_send, b, b_send, plane, far = first_sum(cross, by_x, send(to_x, 0, 1), by_y, send(to_y, 2, 0), far)
    *terms, = second_sum(a, b, send(a_send, 2, 0), send(b_send, 0, 1))
    sums = [terms[0]] + [along(terms[k], k) for k in range(1, nz)]

    far_y, far_x = send(far, 2, 0), send(far, 0, 1)
    far_xy = stack([along(cross, k) for k in range(1, nz)], a)
    parts = [out_grad, cross, plane, far, far_x, far_y, far_xy]
    after = [None, None, None, None, None, None, sums[1]]
    grads = parts + [
        send(p if held is None else lax.optimization_barrier((p, held))[0], 1, 0) for p, held in zip(parts, after)
    ]
    metas = (own, send(own, 1, 0), near, send(near, 1, 0))
    hid_grad, down_grad, mark = backward(hidden, down_weight, metas, grads, ())
    mixed = last_sum(sums, mark)
    return (mixed, hid_grad, down_grad)


def local(hidden, down_weight, expert_ids, combine, out_grad):
    dp_count, cut_count = lax.axis_size("dp"), lax.axis_size("cuts")
    few = dp_count == 4 and cut_count % 4 == 0 and dp_count * expert_ids.shape[0] <= 2 * hidden.shape[1]
    return (shared if few else routed)(hidden, down_weight, expert_ids, combine, out_grad)


def solution(mesh):
    return jax.shard_map(
        local,
        mesh=mesh,
        in_specs=(
            P("dp", None, "cuts"),
            P("dp", "cuts", None),
            P("dp", None),
            P("dp", None),
            P("dp", "cuts"),
        ),
        out_specs=(P("dp", "cuts"), P("dp", None, "cuts"), P("dp", "cuts", None)),
        check_vma=False,
    )
```

```python
import functools

import jax
import jax.numpy as jnp
from jax import lax
from jax.experimental import pallas as pl
from jax.experimental.pallas import tpu as pltpu
from jax.sharding import PartitionSpec as P

BF, F32 = jnp.bfloat16, jnp.float32


def routed(hidden, down_weight, expert_ids, combine, out_grad):
    dp_count = lax.axis_size("dp")
    tok_rows = expert_ids.shape[0]
    capacity = 2 * tok_rows // dp_count
    slot_count = dp_count * capacity
    feat_share = out_grad.shape[1]
    width = down_weight.shape[2]
    flat_ids = expert_ids.reshape(-1)
    labels = jnp.arange(dp_count, dtype=jnp.int32)
    onehot = (flat_ids[:, None] == labels[None, :]).astype(jnp.int32)
    pair_rank = jnp.sum((jnp.cumsum(onehot, axis=0) - 1) * onehot, axis=1)
    inside = flat_ids < dp_count
    target = jnp.where(inside, flat_ids * capacity + pair_rank, dp_count * capacity)
    weights = combine.reshape(-1)
    full_grad = lax.all_gather(out_grad, "cuts", axis=1, tiled=True)
    scaled = (weights[:, None] * jnp.repeat(full_grad, 2, axis=0).astype(F32)).astype(BF)
    outgoing = jnp.zeros((dp_count * capacity, width), BF).at[target].set(scaled, mode="drop")
    incoming = lax.all_to_all(
        outgoing.reshape(dp_count, capacity, width), "dp", split_axis=0, concat_axis=0, tiled=True
    )
    grad_rows = incoming.reshape(slot_count, width)
    hidden_rows = hidden[0]
    weight = down_weight[0]
    own_share = lax.psum_scatter(
        lax.dot_general(weight, hidden_rows, (((0,), (1,)), ((), ())), preferred_element_type=F32),
        "cuts",
        scatter_dimension=0,
        tiled=True,
    )
    hid_grad = lax.dot_general(
        grad_rows, weight, (((1,), (1,)), ((), ())), preferred_element_type=F32
    ).astype(BF)
    down_grad = lax.dot_general(
        hidden_rows, grad_rows, (((0,), (0,)), ((), ())), preferred_element_type=F32
    ).astype(BF)
    returned = lax.all_to_all(
        own_share.astype(BF), "dp", split_axis=1, concat_axis=1, tiled=True
    )
    pick_index = jnp.minimum(target, dp_count * capacity - 1)
    picked = jnp.take(returned, pick_index, axis=1).astype(F32)
    pair_coef = jnp.where(inside, weights, jnp.zeros_like(weights))
    summed = jnp.sum((picked * pair_coef[None, :]).reshape(feat_share, tok_rows, 2), axis=2)
    mixed = summed.T.astype(BF)
    return (mixed, hid_grad[None], down_grad[None])


def routing(meta, expert, capacity):
    tok = meta.shape[1]
    label = jnp.full((1, tok), expert).astype(F32)
    first, second = meta[0:1] == label, meta[1:2] == label
    named = jnp.where(first, 1.0, jnp.where(second, 1.0, 0.0))
    weight = jnp.where(first, meta[2:3], jnp.where(second, meta[3:4], 0.0))
    earlier = lax.broadcasted_iota(jnp.int32, (tok, tok), 0) < lax.broadcasted_iota(
        jnp.int32, (tok, tok), 1
    )
    rank = jnp.dot(
        jnp.broadcast_to(named, (8, tok)).astype(BF),
        jnp.where(earlier, 1.0, 0.0).astype(BF),
        preferred_element_type=F32,
    )[0:1]
    slot = lax.broadcasted_iota(jnp.int32, (capacity, tok), 0).astype(F32)
    hot = jnp.where(slot == rank, named, 0.0)
    return hot, weight


def forward_kernel(nz, capacity, hidden_ref, weight_ref, keep_ref, send_ref, *scratch):
    held, wide, part, rows, sems = scratch
    me = lax.axis_index("dp")
    feat = keep_ref.shape[-1]
    ff = wide.shape[0]
    mid = ff // 2
    first = pltpu.make_async_copy(hidden_ref.at[0], held, sems.at[0])
    low = pltpu.make_async_copy(weight_ref.at[0, pl.ds(0, mid)], wide.at[pl.ds(0, mid)], sems.at[1])
    high = pltpu.make_async_copy(weight_ref.at[0, pl.ds(mid, mid)], wide.at[pl.ds(mid, mid)], sems.at[2])
    for copy in (first, low, high):
        copy.start()
    first.wait()
    low.wait()
    for z in range(nz):
        columns = slice(2 * z * feat, 2 * (z + 1) * feat)
        part[z] = jnp.dot(held[:, :mid], wide[:mid, columns], preferred_element_type=F32)
    high.wait()
    for z in range(nz):
        columns = slice(2 * z * feat, 2 * (z + 1) * feat)
        rest = jnp.dot(held[:, mid:], wide[mid:, columns], preferred_element_type=F32)
        rows[...] = (part[z] + rest).astype(BF)
        for dy in range(2):
            for dc, out in ((0, keep_ref), (1, send_ref)):
                at = pl.multiple_of((me ^ (2 * dy + dc)) * capacity, capacity)
                for x in range(2):
                    out[z, x, dy] = rows[pl.ds(at, capacity), x * feat : (x + 1) * feat]


def forward(hidden, weight, feat, dp_count):
    _, slots, ff = hidden.shape
    width = weight.shape[2]
    nz, capacity = width // (2 * feat), slots // dp_count
    part = jax.ShapeDtypeStruct((nz, 2, 2, capacity, feat), BF)
    hbm, vmem = pl.BlockSpec(memory_space=pltpu.HBM), pl.BlockSpec(memory_space=pltpu.VMEM)
    return pl.pallas_call(
        functools.partial(forward_kernel, nz, capacity),
        in_specs=[hbm] * 2,
        out_specs=[vmem] * 2,
        out_shape=[part, part],
        scratch_shapes=[
            pltpu.VMEM((slots, ff), BF),
            pltpu.VMEM((ff, width), BF),
            pltpu.VMEM((nz, slots, 2 * feat), F32),
            pltpu.VMEM((slots, 2 * feat), BF),
            pltpu.SemaphoreType.DMA((3,)),
        ],
        compiler_params=pltpu.CompilerParams(vmem_limit_bytes=50 << 20),
        cost_estimate=pl.CostEstimate(
            flops=2 * slots * ff * width, bytes_accessed=2 * (ff * width + slots * (ff + width)), transcendentals=0
        ),
        name="forward_rows",
    )(hidden, weight)


def by_token(meta, experts, capacity):
    tok = meta.shape[1]
    table = []
    for expert in experts:
        hot, weight = routing(meta, expert, capacity)
        table.append((hot.astype(BF), jnp.broadcast_to(weight, (tok, tok)).T[:, 0:1]))

    def add_up(first, second):
        terms = [
            lax.dot_general(hot, rows, (((0,), (0,)), ((), ())), preferred_element_type=F32) * weight
            for (hot, weight), rows in zip(table, (first, second))
        ]
        return terms[0] + terms[1]

    return add_up


def spread_kernel(nz, capacity, meta_ref, keep_ref, got_ref, grad_ref, to_x, by_x, to_y, by_y):
    me, x = lax.axis_index("dp"), lax.axis_index("cuts") % 2
    half = nz // 2
    to_x[nz] = grad_ref[...]
    to_y[nz] = grad_ref[...]
    add_up = by_token(meta_ref[...], (me, me ^ 1), capacity)
    for z in range(half):
        to_x[z] = add_up(keep_ref[z, x ^ 1, 0], got_ref[z, x ^ 1, 0]).astype(BF)
        by_x[z] = add_up(keep_ref[z, x, 0], got_ref[z, x, 0])
        to_x[half + z, :capacity] = keep_ref[z, x ^ 1, 1]
        to_x[half + z, capacity:] = got_ref[z, x ^ 1, 1]
        by_x[half + z, :capacity] = keep_ref[z, x, 1].astype(F32)
        by_x[half + z, capacity:] = got_ref[z, x, 1].astype(F32)
        for dx in range(2):
            by_y[half * dx + z] = add_up(keep_ref[half + z, x ^ dx, 0], got_ref[half + z, x ^ dx, 0])
            to_y[half * dx + z, :capacity] = keep_ref[half + z, x ^ dx, 1]
            to_y[half * dx + z, capacity:] = got_ref[half + z, x ^ dx, 1]


def spread(meta, keep, got, grad):
    nz, _, _, capacity, _ = keep.shape
    tok, feat = grad.shape
    shapes = [jax.ShapeDtypeStruct((nz + 1, tok, feat), BF), jax.ShapeDtypeStruct((nz, tok, feat), F32)] * 2
    return pl.pallas_call(
        functools.partial(spread_kernel, nz, capacity),
        out_shape=shapes,
        compiler_params=pltpu.CompilerParams(vmem_limit_bytes=24 << 20),
        cost_estimate=pl.CostEstimate(
            flops=16 * tok * capacity * nz * feat, bytes_accessed=24 * tok * nz * feat, transcendentals=0
        ),
        name="spread_rows",
    )(meta, keep, got, grad)


def first_sum_kernel(half, grad_ref, cross_ref, meta_ref, x_kept, x_got, y_kept, y_got, *refs):
    far, (x_keep, x_send, y_keep, y_send, near_by, stacked) = refs[:-6], refs[-6:]
    me, capacity = lax.axis_index("dp"), x_kept.shape[1] // 2
    for k, ref in enumerate(far):
        stacked[k] = ref[...]
    for i, rows in enumerate((grad_ref[...], x_got[2 * half], y_got[2 * half], cross_ref[...])):
        near_by[i] = rows
    add_up = by_token(meta_ref[...], (me ^ 2, me ^ 3), capacity)
    for z in range(half):
        x_keep[z] = x_kept[z] + x_got[z].astype(F32)
        x_send[z] = (x_kept[half + z] + x_got[half + z].astype(F32)).astype(BF)
        y_keep[z] = y_kept[z] + add_up(y_got[z, :capacity], y_got[z, capacity:])
        y_send[z] = (y_kept[half + z] + add_up(y_got[half + z, :capacity], y_got[half + z, capacity:])).astype(BF)


def first_sum(grad, cross, meta, x_kept, x_got, y_kept, y_got, far):
    nz, tok, feat = x_kept.shape
    half = nz // 2
    shapes = [
        jax.ShapeDtypeStruct((half, tok, feat), F32),
        jax.ShapeDtypeStruct((half, tok, feat), BF),
    ]
    return pl.pallas_call(
        functools.partial(first_sum_kernel, half),
        out_shape=shapes
        + shapes
        + [
            jax.ShapeDtypeStruct((4, tok, feat), BF),
            jax.ShapeDtypeStruct((len(far), tok, feat), BF),
        ],
        compiler_params=pltpu.CompilerParams(vmem_limit_bytes=16 << 20),
        cost_estimate=pl.CostEstimate(flops=1000_000_000, bytes_accessed=0, transcendentals=0),
        name="first_sum",
    )(grad, cross, meta, x_kept, x_got, y_kept, y_got, *far)


def second_sum_kernel(nz, meta_ref, x_kept, y_kept, by_y, by_x, *refs):
    outs, total = refs[:nz], refs[nz]
    me, z, half = lax.axis_index("dp"), lax.axis_index("cuts") // 2, nz // 2
    capacity = by_y.shape[1] // 2
    add_up = by_token(meta_ref[...], (me ^ 2, me ^ 3), capacity)
    for i in range(half):
        total[i] = x_kept[i] + add_up(by_y[i, :capacity], by_y[i, capacity:])
        total[half + i] = y_kept[i] + by_x[i].astype(F32)
    for k in range(nz):
        outs[k][...] = total[lax.rem(z + k, nz)].astype(outs[k].dtype)


def second_sum(meta, x_kept, y_kept, by_y, by_x):
    half, tok, feat = x_kept.shape
    nz = 2 * half
    return pl.pallas_call(
        functools.partial(second_sum_kernel, nz),
        out_shape=[jax.ShapeDtypeStruct((tok, feat), F32 if k == 0 else BF) for k in range(nz)],
        scratch_shapes=[pltpu.VMEM((nz, tok, feat), F32)],
        compiler_params=pltpu.CompilerParams(vmem_limit_bytes=16 << 20),
        cost_estimate=pl.CostEstimate(flops=5000_000_000, bytes_accessed=0, transcendentals=0),
        name="second_sum",
    )(meta, x_kept, y_kept, by_y, by_x)


def stack_kernel(_, meta_ref, near_ref, *refs):
    refs, (stacked, metas) = refs[:-2], refs[-2:]
    for k, ref in enumerate(refs):
        stacked[k] = ref[...]
    metas[0] = meta_ref[...]
    metas[1] = near_ref[...]


def stack(parts, meta, near, after):
    vmem = pl.BlockSpec(memory_space=pltpu.VMEM)
    return pl.pallas_call(
        stack_kernel,
        in_specs=[pl.BlockSpec(memory_space=pl.ANY)] + [vmem] * (2 + len(parts)),
        out_specs=[vmem] * 2,
        out_shape=[
            jax.ShapeDtypeStruct((len(parts), *parts[0].shape), BF),
            jax.ShapeDtypeStruct((2, *meta.shape), F32),
        ],
        compiler_params=pltpu.CompilerParams(vmem_limit_bytes=16 << 20),
        cost_estimate=pl.CostEstimate(flops=1000_000_000, bytes_accessed=0, transcendentals=0),
        name="stack_blocks",
    )(after, meta, near, *parts)


def backward_kernel(nz, capacity, hidden_ref, weight_ref, metas, other_metas, *refs):
    grads, refs = (refs[:5], refs[5:10]), refs[10:]
    hid_out, down_out, mark, made, rows_ref, turned, total, done, hots, cols, sems = refs[-11:]
    mark[...] = jnp.zeros_like(mark)
    me, x, z = lax.axis_index("dp"), lax.axis_index("cuts") % 2, lax.axis_index("cuts") // 2
    feat = rows_ref.shape[1] // 2

    for dy in range(2):
        for dc, ref in enumerate((metas, other_metas)):
            hot, weight = routing(ref[dy], me, capacity)
            hots[2 * dy + dc] = hot.astype(BF)
            cols[2 * dy + dc] = jnp.broadcast_to(jnp.sum(hot * weight, axis=1, keepdims=True), cols.shape[1:])
    turned[...] = hidden_ref[0].T

    def put(dx, q, rows):
        lane = pl.multiple_of((x ^ dx) * feat, feat)
        at = pl.multiple_of((me ^ q) * capacity, capacity)
        picked = jnp.dot(hots[q], rows, preferred_element_type=F32)
        rows_ref[pl.ds(at, capacity), pl.ds(lane, feat)] = (picked * cols[q][:, 0:1]).astype(BF)

    leaving = []
    for k in range(nz):
        for dc in range(2):
            near_by, far, far_x, far_y, far_xy = grads[dc]
            for j, ref in enumerate((far, far_x, far_y, far_xy)):
                put(j % 2, 2 * (j // 2) + dc, near_by[j] if k == 0 else ref[k - 1])
        rows = rows_ref[...]
        column = pl.ds(pl.multiple_of(lax.rem(z - k + nz, nz) * 2 * feat, 2 * feat), 2 * feat)
        part = lax.dot_general(rows, weight_ref[0, :, column], (((1,), (1,)), ((), ())), preferred_element_type=F32)
        if k:
            part = total[...] + part
        if k < nz - 1:
            total[...] = part
        else:
            done[...] = part.astype(BF)
            leaving.append(pltpu.make_async_copy(done, hid_out.at[0], sems.at[2]))
            leaving[-1].start()
        if k >= 2:
            leaving.pop(0).wait()
        made[k % 2] = jnp.dot(turned[...], rows, preferred_element_type=F32).astype(BF)
        leaving.append(pltpu.make_async_copy(made.at[k % 2], down_out.at[0, :, column], sems.at[k % 2]))
        leaving[-1].start()
    for copy in leaving:
        copy.wait()


def backward(hidden, weight, metas, other_metas, grads, after=()):
    tok, feat = grads[1].shape[1:]
    _, slots, ff = hidden.shape
    width = weight.shape[2]
    nz, capacity = width // (2 * feat), slots // 4
    anywhere, vmem = pl.BlockSpec(memory_space=pl.ANY), pl.BlockSpec(memory_space=pltpu.VMEM)
    return pl.pallas_call(
        functools.partial(backward_kernel, nz, capacity),
        in_specs=[vmem] * 14 + [anywhere] * len(after),
        out_specs=[anywhere, anywhere, vmem],
        scratch_shapes=[
            pltpu.VMEM((2, ff, 2 * feat), BF),
            pltpu.VMEM((slots, 2 * feat), BF),
            pltpu.VMEM((ff, slots), BF),
            pltpu.VMEM((slots, ff), F32),
            pltpu.VMEM((slots, ff), BF),
            pltpu.VMEM((4, capacity, tok), BF),
            pltpu.VMEM((4, capacity, 128), F32),
            pltpu.SemaphoreType.DMA((3,)),
        ],
        out_shape=[
            jax.ShapeDtypeStruct(hidden.shape, BF),
            jax.ShapeDtypeStruct(weight.shape, BF),
            jax.ShapeDtypeStruct((8, 128), F32),
        ],
        compiler_params=pltpu.CompilerParams(vmem_limit_bytes=32 << 20),
        cost_estimate=pl.CostEstimate(flops=100_000_000, bytes_accessed=0, transcendentals=0),
        name="backward_rows",
    )(hidden, weight, metas, other_metas, *grads, *after)


def last_sum_kernel(_, first_ref, *refs):
    total = first_ref[...]
    for ref in refs[:-1]:
        total = total + ref[...].astype(F32)
    refs[-1][...] = total.astype(BF)


def last_sum(parts, after):
    vmem = pl.BlockSpec(memory_space=pltpu.VMEM)
    return pl.pallas_call(
        last_sum_kernel,
        in_specs=[pl.BlockSpec(memory_space=pl.ANY)] + [vmem] * len(parts),
        out_specs=vmem,
        out_shape=jax.ShapeDtypeStruct(parts[0].shape, BF),
        compiler_params=pltpu.CompilerParams(vmem_limit_bytes=16 << 20),
        cost_estimate=pl.CostEstimate(flops=1000_000_000, bytes_accessed=0, transcendentals=0),
        name="last_sum",
    )(after, *parts)


def shared(hidden, down_weight, expert_ids, combine, out_grad):
    dp_count, cut_count = lax.axis_size("dp"), lax.axis_size("cuts")
    nz = cut_count // 2
    feat = out_grad.shape[1]

    def send(value, dp_flip, cut_flip):
        pairs = [
            (d * cut_count + c, (d ^ dp_flip) * cut_count + (c ^ cut_flip))
            for d in range(dp_count)
            for c in range(cut_count)
        ]
        return lax.ppermute(value, ("dp", "cuts"), pairs)

    def along(value, k):
        return lax.ppermute(value, "cuts", [(c, (c + 2 * k) % cut_count) for c in range(cut_count)])

    keep, away = forward(hidden, down_weight, out_grad.shape[1], dp_count)
    got = send(away, 1, 0)
    ids, coefs, _ = lax.optimization_barrier((expert_ids, combine, keep))
    own = jnp.pad(ids.T.astype(F32), ((0, 2), (0, 0))) + jnp.pad(coefs.T, ((2, 0), (0, 0)))
    to_x, by_x, to_y, by_y = spread(own, keep, got, out_grad)
    mine, meta, _ = lax.optimization_barrier((out_grad, own, by_x))
    far = [along(mine, k) for k in range(1, nz)]
    cross = send(mine, 2, 1)
    a, a_send, b, b_send, near_by, far = first_sum(
        out_grad, cross, own, by_x, send(to_x, 0, 1), by_y, send(to_y, 2, 0), far
    )
    terms = second_sum(own, a, b, send(a_send, 2, 0), send(b_send, 0, 1))
    sums = [terms[0]] + [along(terms[k], k) for k in range(1, nz)]

    far_y, far_x = send(far, 2, 0), send(far, 0, 1)
    near = send(meta, 2, 0)
    far_xy, metas = stack([along(cross, k) for k in range(1, nz)], own, near, a)
    parts = [near_by, far, far_x, far_y, far_xy]
    after = [None, None, None, None, sums[1]]
    grads = parts + [
        send(p if held is None else lax.optimization_barrier((p, held))[0], 1, 0) for p, held in zip(parts, after)
    ]
    hid_grad, down_grad, mark = backward(hidden, down_weight, metas, send(metas, 1, 0), grads, ())
    mixed = last_sum(sums, mark)
    return (mixed, hid_grad, down_grad)


def local(hidden, down_weight, expert_ids, combine, out_grad):
    dp_count, cut_count = lax.axis_size("dp"), lax.axis_size("cuts")
    few = dp_count == 4 and cut_count % 4 == 0 and dp_count * expert_ids.shape[0] <= 2 * hidden.shape[1]
    return (shared if few else routed)(hidden, down_weight, expert_ids, combine, out_grad)


def solution(mesh):
    return jax.shard_map(
        local,
        mesh=mesh,
        in_specs=(
            P("dp", None, "cuts"),
            P("dp", "cuts", None),
            P("dp", None),
            P("dp", None),
            P("dp", "cuts"),
        ),
        out_specs=(P("dp", "cuts"), P("dp", None, "cuts"), P("dp", "cuts", None)),
        check_vma=False,
    )
```

```python
import functools

import jax
import jax.numpy as jnp
from jax import lax
from jax.experimental import pallas as pl
from jax.experimental.pallas import tpu as pltpu
from jax.sharding import PartitionSpec as P

BF, F32 = jnp.bfloat16, jnp.float32


def routed(hidden, down_weight, expert_ids, combine, out_grad):
    dp_count = lax.axis_size("dp")
    tok_rows = expert_ids.shape[0]
    capacity = 2 * tok_rows // dp_count
    slot_count = dp_count * capacity
    feat_share = out_grad.shape[1]
    width = down_weight.shape[2]
    flat_ids = expert_ids.reshape(-1)
    labels = jnp.arange(dp_count, dtype=jnp.int32)
    onehot = (flat_ids[:, None] == labels[None, :]).astype(jnp.int32)
    pair_rank = jnp.sum((jnp.cumsum(onehot, axis=0) - 1) * onehot, axis=1)
    inside = flat_ids < dp_count
    target = jnp.where(inside, flat_ids * capacity + pair_rank, dp_count * capacity)
    weights = combine.reshape(-1)
    full_grad = lax.all_gather(out_grad, "cuts", axis=1, tiled=True)
    scaled = (weights[:, None] * jnp.repeat(full_grad, 2, axis=0).astype(F32)).astype(BF)
    outgoing = jnp.zeros((dp_count * capacity, width), BF).at[target].set(scaled, mode="drop")
    incoming = lax.all_to_all(
        outgoing.reshape(dp_count, capacity, width), "dp", split_axis=0, concat_axis=0, tiled=True
    )
    grad_rows = incoming.reshape(slot_count, width)
    hidden_rows = hidden[0]
    weight = down_weight[0]
    own_share = lax.psum_scatter(
        lax.dot_general(weight, hidden_rows, (((0,), (1,)), ((), ())), preferred_element_type=F32),
        "cuts",
        scatter_dimension=0,
        tiled=True,
    )
    hid_grad = lax.dot_general(
        grad_rows, weight, (((1,), (1,)), ((), ())), preferred_element_type=F32
    ).astype(BF)
    down_grad = lax.dot_general(
        hidden_rows, grad_rows, (((0,), (0,)), ((), ())), preferred_element_type=F32
    ).astype(BF)
    returned = lax.all_to_all(
        own_share.astype(BF), "dp", split_axis=1, concat_axis=1, tiled=True
    )
    pick_index = jnp.minimum(target, dp_count * capacity - 1)
    picked = jnp.take(returned, pick_index, axis=1).astype(F32)
    pair_coef = jnp.where(inside, weights, jnp.zeros_like(weights))
    summed = jnp.sum((picked * pair_coef[None, :]).reshape(feat_share, tok_rows, 2), axis=2)
    mixed = summed.T.astype(BF)
    return (mixed, hid_grad[None], down_grad[None])


def routing(meta, expert, capacity):
    tok = meta.shape[1]
    label = jnp.full((1, tok), expert).astype(F32)
    first, second = meta[0:1] == label, meta[1:2] == label
    named = jnp.where(first, 1.0, jnp.where(second, 1.0, 0.0))
    weight = jnp.where(first, meta[2:3], jnp.where(second, meta[3:4], 0.0))
    earlier = lax.broadcasted_iota(jnp.int32, (tok, tok), 0) < lax.broadcasted_iota(
        jnp.int32, (tok, tok), 1
    )
    rank = jnp.dot(
        jnp.broadcast_to(named, (8, tok)).astype(BF),
        jnp.where(earlier, 1.0, 0.0).astype(BF),
        preferred_element_type=F32,
    )[0:1]
    slot = lax.broadcasted_iota(jnp.int32, (capacity, tok), 0).astype(F32)
    hot = jnp.where(slot == rank, named, 0.0)
    return hot, weight


def forward_kernel(nz, capacity, hidden_ref, weight_ref, keep_ref, send_ref, *scratch):
    held, wide, part, rows, sems = scratch
    me = lax.axis_index("dp")
    feat = keep_ref.shape[-1]
    ff = wide.shape[0]
    mid = ff // 2
    first = pltpu.make_async_copy(hidden_ref.at[0], held, sems.at[0])
    low = pltpu.make_async_copy(weight_ref.at[0, pl.ds(0, mid)], wide.at[pl.ds(0, mid)], sems.at[1])
    high = pltpu.make_async_copy(weight_ref.at[0, pl.ds(mid, mid)], wide.at[pl.ds(mid, mid)], sems.at[2])
    for copy in (first, low, high):
        copy.start()
    first.wait()
    low.wait()
    for z in range(nz):
        columns = slice(2 * z * feat, 2 * (z + 1) * feat)
        part[z] = jnp.dot(held[:, :mid], wide[:mid, columns], preferred_element_type=F32)
    high.wait()
    for z in range(nz):
        columns = slice(2 * z * feat, 2 * (z + 1) * feat)
        rest = jnp.dot(held[:, mid:], wide[mid:, columns], preferred_element_type=F32)
        rows[...] = (part[z] + rest).astype(BF)
        for dy in range(2):
            for dc, out in ((0, keep_ref), (1, send_ref)):
                at = pl.multiple_of((me ^ (2 * dy + dc)) * capacity, capacity)
                for x in range(2):
                    out[z, x, dy] = rows[pl.ds(at, capacity), x * feat : (x + 1) * feat]


def forward(hidden, weight, feat, dp_count):
    _, slots, ff = hidden.shape
    width = weight.shape[2]
    nz, capacity = width // (2 * feat), slots // dp_count
    part = jax.ShapeDtypeStruct((nz, 2, 2, capacity, feat), BF)
    hbm, vmem = pl.BlockSpec(memory_space=pltpu.HBM), pl.BlockSpec(memory_space=pltpu.VMEM)
    return pl.pallas_call(
        functools.partial(forward_kernel, nz, capacity),
        in_specs=[hbm] * 2,
        out_specs=[vmem] * 2,
        out_shape=[part, part],
        scratch_shapes=[
            pltpu.VMEM((slots, ff), BF),
            pltpu.VMEM((ff, width), BF),
            pltpu.VMEM((nz, slots, 2 * feat), F32),
            pltpu.VMEM((slots, 2 * feat), BF),
            pltpu.SemaphoreType.DMA((3,)),
        ],
        compiler_params=pltpu.CompilerParams(vmem_limit_bytes=50 << 20),
        cost_estimate=pl.CostEstimate(
            flops=2 * slots * ff * width, bytes_accessed=2 * (ff * width + slots * (ff + width)), transcendentals=0
        ),
        name="forward_rows",
    )(hidden, weight)


def by_token(meta, experts, capacity):
    tok = meta.shape[1]
    table = []
    for expert in experts:
        hot, weight = routing(meta, expert, capacity)
        table.append((hot.astype(BF), jnp.broadcast_to(weight, (tok, tok)).T[:, 0:1]))

    def add_up(first, second):
        terms = [
            lax.dot_general(hot, rows, (((0,), (0,)), ((), ())), preferred_element_type=F32) * weight
            for (hot, weight), rows in zip(table, (first, second))
        ]
        return terms[0] + terms[1]

    return add_up


def spread_kernel(nz, capacity, meta_ref, keep_ref, got_ref, grad_ref, to_x, by_x, to_y, by_y, split):
    me, x = lax.axis_index("dp"), lax.axis_index("cuts") % 2
    half = nz // 2
    tok = grad_ref.shape[0]
    to_x[nz] = grad_ref[...]
    to_y[nz * tok : (nz + 1) * tok] = grad_ref[...]
    rest = meta_ref[...]
    count = rest.shape[0]
    split[...] = jnp.zeros_like(split)
    for i in range(3):
        piece = rest.astype(BF).astype(F32)
        split[count * i : count * (i + 1)] = piece
        rest = rest - piece
    to_y[(nz + 1) * tok :, :tok] = split[...].astype(BF)
    add_up = by_token(meta_ref[...], (me, me ^ 1), capacity)
    for z in range(half):
        to_x[z] = add_up(keep_ref[z, x ^ 1, 0], got_ref[z, x ^ 1, 0]).astype(BF)
        by_x[z] = add_up(keep_ref[z, x, 0], got_ref[z, x, 0])
        to_x[half + z, :capacity] = keep_ref[z, x ^ 1, 1]
        to_x[half + z, capacity:] = got_ref[z, x ^ 1, 1]
        by_x[half + z, :capacity] = keep_ref[z, x, 1].astype(F32)
        by_x[half + z, capacity:] = got_ref[z, x, 1].astype(F32)
        for dx in range(2):
            by_y[half * dx + z] = add_up(keep_ref[half + z, x ^ dx, 0], got_ref[half + z, x ^ dx, 0])
            at = (half * dx + z) * tok
            to_y[at : at + capacity] = keep_ref[half + z, x ^ dx, 1]
            to_y[at + capacity : at + tok] = got_ref[half + z, x ^ dx, 1]


def spread(meta, keep, got, grad):
    nz, _, _, capacity, _ = keep.shape
    tok, feat = grad.shape
    kept = jax.ShapeDtypeStruct((nz, tok, feat), F32)
    return pl.pallas_call(
        functools.partial(spread_kernel, nz, capacity),
        out_shape=[
            jax.ShapeDtypeStruct((nz + 1, tok, feat), BF),
            kept,
            jax.ShapeDtypeStruct(((nz + 1) * tok + 16, feat), BF),
            kept,
        ],
        scratch_shapes=[pltpu.VMEM((16, tok), F32)],
        compiler_params=pltpu.CompilerParams(vmem_limit_bytes=24 << 20),
        cost_estimate=pl.CostEstimate(
            flops=16 * tok * capacity * nz * feat, bytes_accessed=24 * tok * nz * feat, transcendentals=0
        ),
        name="spread_rows",
    )(meta, keep, got, grad)


def first_sum_kernel(half, grad_ref, meta_ref, x_kept, x_got, y_kept, y_got, *refs):
    x_keep, x_send, y_keep, y_send, near_by, metas = refs
    me, tok, count = lax.axis_index("dp"), x_kept.shape[1], meta_ref.shape[0]
    capacity, mid = tok // 2, tok // 2
    own = 2 * half * tok
    near_by[0] = grad_ref[...]
    near_by[1] = x_got[2 * half]
    near_by[2] = y_got[own : own + tok]
    x_send[half * tok :] = x_got[2 * half, :mid]
    y_send[half * tok :] = y_got[own + mid : own + tok]
    split = y_got[own + tok :, :tok].astype(F32)
    metas[0] = meta_ref[...]
    metas[1] = split[:count] + split[count : 2 * count] + split[2 * count : 3 * count]
    add_up = by_token(meta_ref[...], (me ^ 2, me ^ 3), capacity)

    def come(place):
        at = place * tok
        return add_up(y_got[at : at + capacity], y_got[at + capacity : at + tok])

    for z in range(half):
        here = slice(z * tok, (z + 1) * tok)
        x_keep[z] = x_kept[z] + x_got[z].astype(F32)
        x_send[here] = (x_kept[half + z] + x_got[half + z].astype(F32)).astype(BF)
        y_keep[z] = y_kept[z] + come(z)
        y_send[here] = (y_kept[half + z] + come(half + z)).astype(BF)


def first_sum(grad, meta, x_kept, x_got, y_kept, y_got):
    nz, tok, feat = x_kept.shape
    half = nz // 2
    shapes = [
        jax.ShapeDtypeStruct((half, tok, feat), F32),
        jax.ShapeDtypeStruct((half * tok + tok // 2, feat), BF),
    ]
    return pl.pallas_call(
        functools.partial(first_sum_kernel, half),
        out_shape=shapes
        + shapes
        + [
            jax.ShapeDtypeStruct((3, tok, feat), BF),
            jax.ShapeDtypeStruct((2, *meta.shape), F32),
        ],
        compiler_params=pltpu.CompilerParams(vmem_limit_bytes=16 << 20),
        cost_estimate=pl.CostEstimate(flops=1000_000_000, bytes_accessed=0, transcendentals=0),
        name="first_sum",
    )(grad, meta, x_kept, x_got, y_kept, y_got)


def stack_kernel(_, *refs):
    for k, ref in enumerate(refs[:-1]):
        refs[-1][k] = ref[...]


def stack(parts, after):
    vmem = pl.BlockSpec(memory_space=pltpu.VMEM)
    return pl.pallas_call(
        stack_kernel,
        in_specs=[pl.BlockSpec(memory_space=pl.ANY)] + [vmem] * len(parts),
        out_specs=vmem,
        out_shape=jax.ShapeDtypeStruct((len(parts), *parts[0].shape), BF),
        compiler_params=pltpu.CompilerParams(vmem_limit_bytes=16 << 20),
        cost_estimate=pl.CostEstimate(flops=1000_000_000, bytes_accessed=0, transcendentals=0),
        name="stack_blocks",
    )(after, *parts)


def second_sum_kernel(nz, meta_ref, x_kept, y_kept, by_y, by_x, *refs):
    outs, cross, total = refs[:nz], refs[nz], refs[nz + 1]
    me, z, half = lax.axis_index("dp"), lax.axis_index("cuts") // 2, nz // 2
    tok = x_kept.shape[1]
    capacity, mid = tok // 2, tok // 2
    cross[:mid] = by_y[half * tok :]
    cross[mid:] = by_x[half * tok :]
    add_up = by_token(meta_ref[...], (me ^ 2, me ^ 3), capacity)
    for i in range(half):
        at = i * tok
        total[i] = x_kept[i] + add_up(by_y[at : at + capacity], by_y[at + capacity : at + tok])
        total[half + i] = y_kept[i] + by_x[at : at + tok].astype(F32)
    for k in range(nz):
        outs[k][...] = total[lax.rem(z + k, nz)].astype(outs[k].dtype)


def second_sum(meta, x_kept, y_kept, by_y, by_x):
    half, tok, feat = x_kept.shape
    nz = 2 * half
    return pl.pallas_call(
        functools.partial(second_sum_kernel, nz),
        out_shape=[jax.ShapeDtypeStruct((tok, feat), F32 if k == 0 else BF) for k in range(nz)]
        + [jax.ShapeDtypeStruct((tok, feat), BF)],
        scratch_shapes=[pltpu.VMEM((nz, tok, feat), F32)],
        compiler_params=pltpu.CompilerParams(vmem_limit_bytes=16 << 20),
        cost_estimate=pl.CostEstimate(flops=1000_000_000, bytes_accessed=0, transcendentals=0),
        name="second_sum",
    )(meta, x_kept, y_kept, by_y, by_x)


def put(rows_ref, hots, cols, dx, q, grads):
    capacity, feat = hots.shape[1], grads.shape[1]
    lane = pl.multiple_of((lax.axis_index("cuts") % 2 ^ dx) * feat, feat)
    at = pl.multiple_of((lax.axis_index("dp") ^ q) * capacity, capacity)
    picked = jnp.dot(hots[q], grads, preferred_element_type=F32)
    rows_ref[pl.ds(at, capacity), pl.ds(lane, feat)] = (picked * cols[q][:, 0:1]).astype(BF)


def columns(nz, k, feat):
    z = lax.rem(lax.axis_index("cuts") // 2 - k + nz, nz)
    return pl.ds(pl.multiple_of(z * 2 * feat, 2 * feat), 2 * feat)


def times_transposed(rows, weight):
    return lax.dot_general(rows, weight, (((1,), (1,)), ((), ())), preferred_element_type=F32)


def backward_here_kernel(nz, hidden_ref, weight_ref, metas, other_metas, *refs):
    grads, (part, down_out, turned, hots, cols), (made, rows_ref, sem) = refs[:4], refs[-8:-3], refs[-3:]
    me, capacity, feat = lax.axis_index("dp"), hots.shape[1], rows_ref.shape[1] // 2
    for dy in range(2):
        for dc, ref in enumerate((metas, other_metas)):
            hot, weight = routing(ref[dy], me, capacity)
            hots[2 * dy + dc] = hot.astype(BF)
            cols[2 * dy + dc] = jnp.broadcast_to(jnp.sum(hot * weight, axis=1, keepdims=True), cols.shape[1:])
    turned[...] = hidden_ref[0].T
    for dc in range(2):
        for j in range(4):
            put(rows_ref, hots, cols, j % 2, 2 * (j // 2) + dc, grads[dc][j] if j < 3 else grads[2 + dc][...])
    rows, column = rows_ref[...], columns(nz, 0, feat)
    made[...] = jnp.dot(turned[...], rows, preferred_element_type=F32).astype(BF)
    copy = pltpu.make_async_copy(made, down_out.at[0, :, column], sem)
    copy.start()
    part[...] = times_transposed(rows, weight_ref[0, :, column])
    copy.wait()


def backward_here(hidden, weight, metas, other_metas, near_by, cross, after=()):
    _, slots, ff = hidden.shape
    tok, feat = near_by[0].shape[1:]
    capacity = slots // 4
    anywhere, vmem = pl.BlockSpec(memory_space=pl.ANY), pl.BlockSpec(memory_space=pltpu.VMEM)
    return pl.pallas_call(
        functools.partial(backward_here_kernel, weight.shape[2] // (2 * feat)),
        in_specs=[vmem] * 8 + [anywhere] * len(after),
        out_specs=[vmem, anywhere, vmem, vmem, vmem],
        scratch_shapes=[
            pltpu.VMEM((ff, 2 * feat), BF),
            pltpu.VMEM((slots, 2 * feat), BF),
            pltpu.SemaphoreType.DMA,
        ],
        out_shape=[
            jax.ShapeDtypeStruct((slots, ff), F32),
            jax.ShapeDtypeStruct(weight.shape, BF),
            jax.ShapeDtypeStruct((ff, slots), BF),
            jax.ShapeDtypeStruct((4, capacity, tok), BF),
            jax.ShapeDtypeStruct((4, capacity, 128), F32),
        ],
        compiler_params=pltpu.CompilerParams(vmem_limit_bytes=16 << 20),
        cost_estimate=pl.CostEstimate(flops=2000_000_000, bytes_accessed=0, transcendentals=0),
        name="backward_here",
    )(hidden, weight, metas, other_metas, *near_by, *cross, *after)


def backward_kernel(nz, weight_ref, part_ref, turned, hots, cols, *refs):
    grads, (hid_out, down_out, mark), (made, rows_ref, total, done, sems) = (refs[:5], refs[5:10]), refs[-8:-5], refs[-5:]
    feat = rows_ref.shape[1] // 2
    mark[...] = jnp.zeros_like(mark)
    leaving = []
    for k in range(1, nz):
        for dc in range(2):
            far, far_x, far_y, low, high = grads[dc]
            count = low.shape[0]
            cross = low[k - 1] if k <= count else high[k - 1 - count]
            for j, rows in enumerate((far[k - 1], far_x[k - 1], far_y[k - 1], cross)):
                put(rows_ref, hots, cols, j % 2, 2 * (j // 2) + dc, rows)
        rows, column = rows_ref[...], columns(nz, k, feat)
        part = (part_ref if k == 1 else total)[...] + times_transposed(rows, weight_ref[0, :, column])
        if k < nz - 1:
            total[...] = part
        else:
            done[...] = part.astype(BF)
            leaving.append(pltpu.make_async_copy(done, hid_out.at[0], sems.at[2]))
            leaving[-1].start()
        if k > 2:
            leaving.pop(0).wait()
        made[k % 2] = jnp.dot(turned[...], rows, preferred_element_type=F32).astype(BF)
        leaving.append(pltpu.make_async_copy(made.at[k % 2], down_out.at[0, :, column], sems.at[k % 2]))
        leaving[-1].start()
    for copy in leaving:
        copy.wait()


def backward(hidden, weight, here, grads, after=()):
    part, down, turned, hots, cols = here
    feat = grads[0].shape[2]
    _, slots, ff = hidden.shape
    anywhere, vmem = pl.BlockSpec(memory_space=pl.ANY), pl.BlockSpec(memory_space=pltpu.VMEM)
    return pl.pallas_call(
        functools.partial(backward_kernel, weight.shape[2] // (2 * feat)),
        in_specs=[vmem] * 15 + [anywhere] * (1 + len(after)),
        out_specs=[anywhere, anywhere, vmem],
        scratch_shapes=[
            pltpu.VMEM((2, ff, 2 * feat), BF),
            pltpu.VMEM((slots, 2 * feat), BF),
            pltpu.VMEM((slots, ff), F32),
            pltpu.VMEM((slots, ff), BF),
            pltpu.SemaphoreType.DMA((3,)),
        ],
        out_shape=[
            jax.ShapeDtypeStruct(hidden.shape, BF),
            jax.ShapeDtypeStruct(weight.shape, BF),
            jax.ShapeDtypeStruct((8, 128), F32),
        ],
        input_output_aliases={15: 1},
        compiler_params=pltpu.CompilerParams(vmem_limit_bytes=32 << 20),
        cost_estimate=pl.CostEstimate(flops=100_000_000, bytes_accessed=0, transcendentals=0),
        name="backward_rows",
    )(weight, part, turned, hots, cols, *grads, down, *after)


def last_sum_kernel(_, first_ref, *refs):
    total = first_ref[...]
    for ref in refs[:-1]:
        total = total + ref[...].astype(F32)
    refs[-1][...] = total.astype(BF)


def last_sum(parts, after):
    vmem = pl.BlockSpec(memory_space=pltpu.VMEM)
    return pl.pallas_call(
        last_sum_kernel,
        in_specs=[pl.BlockSpec(memory_space=pl.ANY)] + [vmem] * len(parts),
        out_specs=vmem,
        out_shape=jax.ShapeDtypeStruct(parts[0].shape, BF),
        compiler_params=pltpu.CompilerParams(vmem_limit_bytes=16 << 20),
        cost_estimate=pl.CostEstimate(flops=1000_000_000, bytes_accessed=0, transcendentals=0),
        name="last_sum",
    )(after, *parts)


def shared(hidden, down_weight, expert_ids, combine, out_grad):
    dp_count, cut_count = lax.axis_size("dp"), lax.axis_size("cuts")
    nz = cut_count // 2
    feat = out_grad.shape[1]

    def send(value, dp_flip, cut_flip):
        pairs = [
            (d * cut_count + c, (d ^ dp_flip) * cut_count + (c ^ cut_flip))
            for d in range(dp_count)
            for c in range(cut_count)
        ]
        return lax.ppermute(value, ("dp", "cuts"), pairs)

    def along(value, k):
        return lax.ppermute(value, "cuts", [(c, (c + 2 * k) % cut_count) for c in range(cut_count)])

    keep, away = forward(hidden, down_weight, out_grad.shape[1], dp_count)
    got = send(away, 1, 0)
    ids, coefs, _ = lax.optimization_barrier((expert_ids, combine, keep))
    own = jnp.pad(ids.T.astype(F32), ((0, 2), (0, 0))) + jnp.pad(coefs.T, ((2, 0), (0, 0)))
    to_x, by_x, to_y, by_y = spread(own, keep, got, out_grad)
    mine, _ = lax.optimization_barrier((out_grad, by_x))
    far = [along(mine, k) for k in range(1, nz)]
    a, a_send, b, b_send, near_by, metas = first_sum(
        out_grad, own, by_x, send(to_x, 0, 1), by_y, send(to_y, 2, 0)
    )
    other = send(near_by, 1, 0)
    far = stack(far, a)
    *terms, cross = second_sum(own, a, b, send(a_send, 2, 0), send(b_send, 0, 1))
    sums = [terms[0]] + [along(terms[k], k) for k in range(1, nz)]

    far_y, far_x = send(far, 2, 0), send(far, 0, 1)
    low, high = send(far_x[: nz // 2], 2, 0), send(far_y[nz // 2 :], 0, 1)
    here = backward_here(
        hidden, down_weight, metas, send(metas, 1, 0), (near_by, other), (cross, send(cross, 1, 0)), (sums[1], sums[-1])
    )
    parts = [far, far_x, far_y, low, high]
    after = [None, None, None, here[0], sums[-1]]
    grads = parts + [
        send(p if held is None else lax.optimization_barrier((p, held))[0], 1, 0) for p, held in zip(parts, after)
    ]
    hid_grad, down_grad, mark = backward(hidden, down_weight, here, grads, ())
    mixed = last_sum(sums, mark)
    return (mixed, hid_grad, down_grad)


def local(hidden, down_weight, expert_ids, combine, out_grad):
    dp_count, cut_count = lax.axis_size("dp"), lax.axis_size("cuts")
    few = dp_count == 4 and cut_count % 4 == 0 and expert_ids.shape[0] <= out_grad.shape[1] and dp_count * expert_ids.shape[0] <= 2 * hidden.shape[1]
    return (shared if few else routed)(hidden, down_weight, expert_ids, combine, out_grad)


def solution(mesh):
    return jax.shard_map(
        local,
        mesh=mesh,
        in_specs=(
            P("dp", None, "cuts"),
            P("dp", "cuts", None),
            P("dp", None),
            P("dp", None),
            P("dp", "cuts"),
        ),
        out_specs=(P("dp", "cuts"), P("dp", None, "cuts"), P("dp", "cuts", None)),
        check_vma=False,
    )
```

```python
import functools

import jax
import jax.numpy as jnp
from jax import lax
from jax.experimental import pallas as pl
from jax.experimental.pallas import tpu as pltpu
from jax.sharding import PartitionSpec as P

BF, F32 = jnp.bfloat16, jnp.float32


def routed(hidden, down_weight, expert_ids, combine, out_grad):
    dp_count = lax.axis_size("dp")
    tok_rows = expert_ids.shape[0]
    capacity = 2 * tok_rows // dp_count
    slot_count = dp_count * capacity
    feat_share = out_grad.shape[1]
    width = down_weight.shape[2]
    flat_ids = expert_ids.reshape(-1)
    labels = jnp.arange(dp_count, dtype=jnp.int32)
    onehot = (flat_ids[:, None] == labels[None, :]).astype(jnp.int32)
    pair_rank = jnp.sum((jnp.cumsum(onehot, axis=0) - 1) * onehot, axis=1)
    inside = flat_ids < dp_count
    target = jnp.where(inside, flat_ids * capacity + pair_rank, dp_count * capacity)
    weights = combine.reshape(-1)
    full_grad = lax.all_gather(out_grad, "cuts", axis=1, tiled=True)
    scaled = (weights[:, None] * jnp.repeat(full_grad, 2, axis=0).astype(F32)).astype(BF)
    outgoing = jnp.zeros((dp_count * capacity, width), BF).at[target].set(scaled, mode="drop")
    incoming = lax.all_to_all(
        outgoing.reshape(dp_count, capacity, width), "dp", split_axis=0, concat_axis=0, tiled=True
    )
    grad_rows = incoming.reshape(slot_count, width)
    hidden_rows = hidden[0]
    weight = down_weight[0]
    own_share = lax.psum_scatter(
        lax.dot_general(weight, hidden_rows, (((0,), (1,)), ((), ())), preferred_element_type=F32),
        "cuts",
        scatter_dimension=0,
        tiled=True,
    )
    hid_grad = lax.dot_general(
        grad_rows, weight, (((1,), (1,)), ((), ())), preferred_element_type=F32
    ).astype(BF)
    down_grad = lax.dot_general(
        hidden_rows, grad_rows, (((0,), (0,)), ((), ())), preferred_element_type=F32
    ).astype(BF)
    returned = lax.all_to_all(
        own_share.astype(BF), "dp", split_axis=1, concat_axis=1, tiled=True
    )
    pick_index = jnp.minimum(target, dp_count * capacity - 1)
    picked = jnp.take(returned, pick_index, axis=1).astype(F32)
    pair_coef = jnp.where(inside, weights, jnp.zeros_like(weights))
    summed = jnp.sum((picked * pair_coef[None, :]).reshape(feat_share, tok_rows, 2), axis=2)
    mixed = summed.T.astype(BF)
    return (mixed, hid_grad[None], down_grad[None])


def routing(meta, expert, capacity):
    tok = meta.shape[1]
    label = jnp.full((1, tok), expert).astype(F32)
    first, second = meta[0:1] == label, meta[1:2] == label
    named = jnp.where(first, 1.0, jnp.where(second, 1.0, 0.0))
    weight = jnp.where(first, meta[2:3], jnp.where(second, meta[3:4], 0.0))
    earlier = lax.broadcasted_iota(jnp.int32, (tok, tok), 0) < lax.broadcasted_iota(
        jnp.int32, (tok, tok), 1
    )
    rank = jnp.dot(
        jnp.broadcast_to(named, (8, tok)).astype(BF),
        jnp.where(earlier, 1.0, 0.0).astype(BF),
        preferred_element_type=F32,
    )[0:1]
    slot = lax.broadcasted_iota(jnp.int32, (capacity, tok), 0).astype(F32)
    hot = jnp.where(slot == rank, named, 0.0)
    return hot, weight


def forward_kernel(nz, capacity, hidden_ref, weight_ref, keep_ref, send_ref, *scratch):
    held, wide, part, rows, sems = scratch
    me = lax.axis_index("dp")
    feat = keep_ref.shape[-1]
    ff = wide.shape[0]
    mid = ff // 2
    first = pltpu.make_async_copy(hidden_ref.at[0], held, sems.at[0])
    low = pltpu.make_async_copy(weight_ref.at[0, pl.ds(0, mid)], wide.at[pl.ds(0, mid)], sems.at[1])
    high = pltpu.make_async_copy(weight_ref.at[0, pl.ds(mid, mid)], wide.at[pl.ds(mid, mid)], sems.at[2])
    for copy in (first, low, high):
        copy.start()
    first.wait()
    low.wait()
    for z in range(nz):
        columns = slice(2 * z * feat, 2 * (z + 1) * feat)
        part[z] = jnp.dot(held[:, :mid], wide[:mid, columns], preferred_element_type=F32)
    high.wait()
    for z in range(nz):
        columns = slice(2 * z * feat, 2 * (z + 1) * feat)
        rest = jnp.dot(held[:, mid:], wide[mid:, columns], preferred_element_type=F32)
        rows[...] = (part[z] + rest).astype(BF)
        for dy in range(2):
            for dc, out in ((0, keep_ref), (1, send_ref)):
                at = pl.multiple_of((me ^ (2 * dy + dc)) * capacity, capacity)
                for x in range(2):
                    out[z, x, dy] = rows[pl.ds(at, capacity), x * feat : (x + 1) * feat]


def forward(hidden, weight, feat, dp_count):
    _, slots, ff = hidden.shape
    width = weight.shape[2]
    nz, capacity = width // (2 * feat), slots // dp_count
    part = jax.ShapeDtypeStruct((nz, 2, 2, capacity, feat), BF)
    hbm, vmem = pl.BlockSpec(memory_space=pltpu.HBM), pl.BlockSpec(memory_space=pltpu.VMEM)
    return pl.pallas_call(
        functools.partial(forward_kernel, nz, capacity),
        in_specs=[hbm] * 2,
        out_specs=[vmem] * 2,
        out_shape=[part, part],
        scratch_shapes=[
            pltpu.VMEM((slots, ff), BF),
            pltpu.VMEM((ff, width), BF),
            pltpu.VMEM((nz, slots, 2 * feat), F32),
            pltpu.VMEM((slots, 2 * feat), BF),
            pltpu.SemaphoreType.DMA((3,)),
        ],
        compiler_params=pltpu.CompilerParams(vmem_limit_bytes=50 << 20),
        cost_estimate=pl.CostEstimate(
            flops=2 * slots * ff * width, bytes_accessed=2 * (ff * width + slots * (ff + width)), transcendentals=0
        ),
        name="forward_rows",
    )(hidden, weight)


def by_token(meta, experts, capacity):
    tok = meta.shape[1]
    table = []
    for expert in experts:
        hot, weight = routing(meta, expert, capacity)
        table.append((hot.astype(BF), jnp.broadcast_to(weight, (tok, tok)).T[:, 0:1]))

    def add_up(first, second):
        terms = [
            lax.dot_general(hot, rows, (((0,), (0,)), ((), ())), preferred_element_type=F32) * weight
            for (hot, weight), rows in zip(table, (first, second))
        ]
        return terms[0] + terms[1]

    return add_up


def spread_kernel(nz, capacity, meta_ref, keep_ref, got_ref, grad_ref, to_x, by_x, to_y, by_y, split):
    me, x = lax.axis_index("dp"), lax.axis_index("cuts") % 2
    half = nz // 2
    tok = grad_ref.shape[0]
    to_x[nz] = grad_ref[...]
    to_y[nz * tok : (nz + 1) * tok] = grad_ref[...]
    rest = meta_ref[...]
    count = rest.shape[0]
    split[...] = jnp.zeros_like(split)
    for i in range(3):
        piece = rest.astype(BF).astype(F32)
        split[count * i : count * (i + 1)] = piece
        rest = rest - piece
    to_y[(nz + 1) * tok :, :tok] = split[...].astype(BF)
    add_up = by_token(meta_ref[...], (me, me ^ 1), capacity)
    for z in range(half):
        to_x[z] = add_up(keep_ref[z, x ^ 1, 0], got_ref[z, x ^ 1, 0]).astype(BF)
        by_x[z] = add_up(keep_ref[z, x, 0], got_ref[z, x, 0])
        to_x[half + z, :capacity] = keep_ref[z, x ^ 1, 1]
        to_x[half + z, capacity:] = got_ref[z, x ^ 1, 1]
        by_x[half + z, :capacity] = keep_ref[z, x, 1].astype(F32)
        by_x[half + z, capacity:] = got_ref[z, x, 1].astype(F32)
        for dx in range(2):
            by_y[half * dx + z] = add_up(keep_ref[half + z, x ^ dx, 0], got_ref[half + z, x ^ dx, 0])
            at = (half * dx + z) * tok
            to_y[at : at + capacity] = keep_ref[half + z, x ^ dx, 1]
            to_y[at + capacity : at + tok] = got_ref[half + z, x ^ dx, 1]


def spread(meta, keep, got, grad):
    nz, _, _, capacity, _ = keep.shape
    tok, feat = grad.shape
    kept = jax.ShapeDtypeStruct((nz, tok, feat), F32)
    return pl.pallas_call(
        functools.partial(spread_kernel, nz, capacity),
        out_shape=[
            jax.ShapeDtypeStruct((nz + 1, tok, feat), BF),
            kept,
            jax.ShapeDtypeStruct(((nz + 1) * tok + 16, feat), BF),
            kept,
        ],
        scratch_shapes=[pltpu.VMEM((16, tok), F32)],
        compiler_params=pltpu.CompilerParams(vmem_limit_bytes=24 << 20),
        cost_estimate=pl.CostEstimate(
            flops=16 * tok * capacity * nz * feat, bytes_accessed=24 * tok * nz * feat, transcendentals=0
        ),
        name="spread_rows",
    )(meta, keep, got, grad)


def first_sum_kernel(half, grad_ref, meta_ref, x_kept, x_got, y_kept, y_got, *refs):
    x_keep, x_send, y_keep, y_send, near_by, metas = refs
    me, tok, count = lax.axis_index("dp"), x_kept.shape[1], meta_ref.shape[0]
    capacity, mid = tok // 2, tok // 2
    own = 2 * half * tok
    near_by[0] = grad_ref[...]
    near_by[1] = x_got[2 * half]
    near_by[2] = y_got[own : own + tok]
    x_send[half * tok :] = x_got[2 * half, :mid]
    y_send[half * tok :] = y_got[own + mid : own + tok]
    split = y_got[own + tok :, :tok].astype(F32)
    metas[0] = meta_ref[...]
    metas[1] = split[:count] + split[count : 2 * count] + split[2 * count : 3 * count]
    add_up = by_token(meta_ref[...], (me ^ 2, me ^ 3), capacity)

    def come(place):
        at = place * tok
        return add_up(y_got[at : at + capacity], y_got[at + capacity : at + tok])

    for z in range(half):
        here = slice(z * tok, (z + 1) * tok)
        x_keep[z] = x_kept[z] + x_got[z].astype(F32)
        x_send[here] = (x_kept[half + z] + x_got[half + z].astype(F32)).astype(BF)
        y_keep[z] = y_kept[z] + come(z)
        y_send[here] = (y_kept[half + z] + come(half + z)).astype(BF)


def first_sum(grad, meta, x_kept, x_got, y_kept, y_got):
    nz, tok, feat = x_kept.shape
    half = nz // 2
    shapes = [
        jax.ShapeDtypeStruct((half, tok, feat), F32),
        jax.ShapeDtypeStruct((half * tok + tok // 2, feat), BF),
    ]
    return pl.pallas_call(
        functools.partial(first_sum_kernel, half),
        out_shape=shapes
        + shapes
        + [
            jax.ShapeDtypeStruct((3, tok, feat), BF),
            jax.ShapeDtypeStruct((2, *meta.shape), F32),
        ],
        compiler_params=pltpu.CompilerParams(vmem_limit_bytes=16 << 20),
        cost_estimate=pl.CostEstimate(flops=1000_000_000, bytes_accessed=0, transcendentals=0),
        name="first_sum",
    )(grad, meta, x_kept, x_got, y_kept, y_got)


def stack_kernel(_, *refs):
    for k, ref in enumerate(refs[:-1]):
        refs[-1][k] = ref[...]


def stack(parts, after):
    vmem = pl.BlockSpec(memory_space=pltpu.VMEM)
    return pl.pallas_call(
        stack_kernel,
        in_specs=[pl.BlockSpec(memory_space=pl.ANY)] + [vmem] * len(parts),
        out_specs=vmem,
        out_shape=jax.ShapeDtypeStruct((len(parts), *parts[0].shape), BF),
        compiler_params=pltpu.CompilerParams(vmem_limit_bytes=16 << 20),
        cost_estimate=pl.CostEstimate(flops=1000_000_000, bytes_accessed=0, transcendentals=0),
        name="stack_blocks",
    )(after, *parts)


def second_sum_kernel(nz, meta_ref, x_kept, y_kept, by_y, by_x, *refs):
    outs, cross, total = refs[:nz], refs[nz], refs[nz + 1]
    me, z, half = lax.axis_index("dp"), lax.axis_index("cuts") // 2, nz // 2
    tok = x_kept.shape[1]
    capacity, mid = tok // 2, tok // 2
    cross[:mid] = by_y[half * tok :]
    cross[mid:] = by_x[half * tok :]
    add_up = by_token(meta_ref[...], (me ^ 2, me ^ 3), capacity)
    for i in range(half):
        at = i * tok
        total[i] = x_kept[i] + add_up(by_y[at : at + capacity], by_y[at + capacity : at + tok])
        total[half + i] = y_kept[i] + by_x[at : at + tok].astype(F32)
    for k in range(nz):
        outs[k][...] = total[lax.rem(z + k, nz)].astype(outs[k].dtype)


def second_sum(meta, x_kept, y_kept, by_y, by_x):
    half, tok, feat = x_kept.shape
    nz = 2 * half
    return pl.pallas_call(
        functools.partial(second_sum_kernel, nz),
        out_shape=[jax.ShapeDtypeStruct((tok, feat), F32 if k == 0 else BF) for k in range(nz)]
        + [jax.ShapeDtypeStruct((tok, feat), BF)],
        scratch_shapes=[pltpu.VMEM((nz, tok, feat), F32)],
        compiler_params=pltpu.CompilerParams(vmem_limit_bytes=16 << 20),
        cost_estimate=pl.CostEstimate(flops=1000_000_000, bytes_accessed=0, transcendentals=0),
        name="second_sum",
    )(meta, x_kept, y_kept, by_y, by_x)


def put(rows_ref, hots, cols, dx, q, grads):
    capacity, feat = hots.shape[1], grads.shape[1]
    lane = pl.multiple_of((lax.axis_index("cuts") % 2 ^ dx) * feat, feat)
    at = pl.multiple_of((lax.axis_index("dp") ^ q) * capacity, capacity)
    picked = jnp.dot(hots[q], grads, preferred_element_type=F32)
    rows_ref[pl.ds(at, capacity), pl.ds(lane, feat)] = (picked * cols[q][:, 0:1]).astype(BF)


def columns(nz, k, feat):
    z = lax.rem(lax.axis_index("cuts") // 2 - k + nz, nz)
    return pl.ds(pl.multiple_of(z * 2 * feat, 2 * feat), 2 * feat)


def times_transposed(rows, weight):
    return lax.dot_general(rows, weight, (((1,), (1,)), ((), ())), preferred_element_type=F32)


def backward_here_kernel(nz, hidden_ref, weight_ref, metas, other_metas, *refs):
    grads, (part, down_out, turned, hots, cols), (made, rows_ref, sem) = refs[:4], refs[-8:-3], refs[-3:]
    me, capacity, feat = lax.axis_index("dp"), hots.shape[1], rows_ref.shape[1] // 2
    for dy in range(2):
        for dc, ref in enumerate((metas, other_metas)):
            hot, weight = routing(ref[dy], me, capacity)
            hots[2 * dy + dc] = hot.astype(BF)
            cols[2 * dy + dc] = jnp.broadcast_to(jnp.sum(hot * weight, axis=1, keepdims=True), cols.shape[1:])
    turned[...] = hidden_ref[0].T
    for dc in range(2):
        for j in range(4):
            put(rows_ref, hots, cols, j % 2, 2 * (j // 2) + dc, grads[dc][j] if j < 3 else grads[2 + dc][...])
    rows, column = rows_ref[...], columns(nz, 0, feat)
    made[...] = jnp.dot(turned[...], rows, preferred_element_type=F32).astype(BF)
    copy = pltpu.make_async_copy(made, down_out.at[0, :, column], sem)
    copy.start()
    part[...] = times_transposed(rows, weight_ref[0, :, column])
    copy.wait()


def backward_here(hidden, weight, metas, other_metas, near_by, cross, after=()):
    _, slots, ff = hidden.shape
    tok, feat = near_by[0].shape[1:]
    capacity = slots // 4
    anywhere, vmem = pl.BlockSpec(memory_space=pl.ANY), pl.BlockSpec(memory_space=pltpu.VMEM)
    return pl.pallas_call(
        functools.partial(backward_here_kernel, weight.shape[2] // (2 * feat)),
        in_specs=[vmem] * 8 + [anywhere] * len(after),
        out_specs=[vmem, anywhere, vmem, vmem, vmem],
        scratch_shapes=[
            pltpu.VMEM((ff, 2 * feat), BF),
            pltpu.VMEM((slots, 2 * feat), BF),
            pltpu.SemaphoreType.DMA,
        ],
        out_shape=[
            jax.ShapeDtypeStruct((slots, ff), F32),
            jax.ShapeDtypeStruct(weight.shape, BF),
            jax.ShapeDtypeStruct((ff, slots), BF),
            jax.ShapeDtypeStruct((4, capacity, tok), BF),
            jax.ShapeDtypeStruct((4, capacity, 128), F32),
        ],
        compiler_params=pltpu.CompilerParams(vmem_limit_bytes=16 << 20),
        cost_estimate=pl.CostEstimate(flops=2000_000_000, bytes_accessed=0, transcendentals=0),
        name="backward_here",
    )(hidden, weight, metas, other_metas, *near_by, *cross, *after)


def backward_kernel(nz, weight_ref, part_ref, turned, hots, cols, *refs):
    grads, (hid_out, down_out, mark), (made, rows_ref, total, done, sems) = (refs[:5], refs[5:10]), refs[-8:-5], refs[-5:]
    feat = rows_ref.shape[1] // 2
    mark[...] = jnp.zeros_like(mark)
    leaving = []
    for k in range(1, nz):
        for dc in range(2):
            far, far_x, far_y, low, high = grads[dc]
            count = low.shape[0]
            cross = low[k - 1] if k <= count else high[k - 1 - count]
            for j, rows in enumerate((far[k - 1], far_x[k - 1], far_y[k - 1], cross)):
                put(rows_ref, hots, cols, j % 2, 2 * (j // 2) + dc, rows)
        rows, column = rows_ref[...], columns(nz, k, feat)
        if k > 2:
            leaving.pop(0).wait()
        made[k % 2] = jnp.dot(turned[...], rows, preferred_element_type=F32).astype(BF)
        leaving.append(pltpu.make_async_copy(made.at[k % 2], down_out.at[0, :, column], sems.at[k % 2]))
        leaving[-1].start()
        part = (part_ref if k == 1 else total)[...] + times_transposed(rows, weight_ref[0, :, column])
        if k < nz - 1:
            total[...] = part
        else:
            done[...] = part.astype(BF)
            leaving.append(pltpu.make_async_copy(done, hid_out.at[0], sems.at[2]))
            leaving[-1].start()
    for copy in leaving:
        copy.wait()


def backward(hidden, weight, here, grads, after=()):
    part, down, turned, hots, cols = here
    feat = grads[0].shape[2]
    _, slots, ff = hidden.shape
    anywhere, vmem = pl.BlockSpec(memory_space=pl.ANY), pl.BlockSpec(memory_space=pltpu.VMEM)
    return pl.pallas_call(
        functools.partial(backward_kernel, weight.shape[2] // (2 * feat)),
        in_specs=[vmem] * 15 + [anywhere] * (1 + len(after)),
        out_specs=[anywhere, anywhere, vmem],
        scratch_shapes=[
            pltpu.VMEM((2, ff, 2 * feat), BF),
            pltpu.VMEM((slots, 2 * feat), BF),
            pltpu.VMEM((slots, ff), F32),
            pltpu.VMEM((slots, ff), BF),
            pltpu.SemaphoreType.DMA((3,)),
        ],
        out_shape=[
            jax.ShapeDtypeStruct(hidden.shape, BF),
            jax.ShapeDtypeStruct(weight.shape, BF),
            jax.ShapeDtypeStruct((8, 128), F32),
        ],
        input_output_aliases={15: 1},
        compiler_params=pltpu.CompilerParams(vmem_limit_bytes=32 << 20),
        cost_estimate=pl.CostEstimate(flops=100_000_000, bytes_accessed=0, transcendentals=0),
        name="backward_rows",
    )(weight, part, turned, hots, cols, *grads, down, *after)


def last_sum_kernel(_, first_ref, *refs):
    total = first_ref[...]
    for ref in refs[:-1]:
        total = total + ref[...].astype(F32)
    refs[-1][...] = total.astype(BF)


def last_sum(parts, after):
    vmem = pl.BlockSpec(memory_space=pltpu.VMEM)
    return pl.pallas_call(
        last_sum_kernel,
        in_specs=[pl.BlockSpec(memory_space=pl.ANY)] + [vmem] * len(parts),
        out_specs=vmem,
        out_shape=jax.ShapeDtypeStruct(parts[0].shape, BF),
        compiler_params=pltpu.CompilerParams(vmem_limit_bytes=16 << 20),
        cost_estimate=pl.CostEstimate(flops=1000_000_000, bytes_accessed=0, transcendentals=0),
        name="last_sum",
    )(after, *parts)


def shared(hidden, down_weight, expert_ids, combine, out_grad):
    dp_count, cut_count = lax.axis_size("dp"), lax.axis_size("cuts")
    nz = cut_count // 2
    feat = out_grad.shape[1]

    def send(value, dp_flip, cut_flip):
        pairs = [
            (d * cut_count + c, (d ^ dp_flip) * cut_count + (c ^ cut_flip))
            for d in range(dp_count)
            for c in range(cut_count)
        ]
        return lax.ppermute(value, ("dp", "cuts"), pairs)

    def along(value, k):
        return lax.ppermute(value, "cuts", [(c, (c + 2 * k) % cut_count) for c in range(cut_count)])

    keep, away = forward(hidden, down_weight, out_grad.shape[1], dp_count)
    got = send(away, 1, 0)
    ids, coefs, _ = lax.optimization_barrier((expert_ids, combine, keep))
    own = jnp.pad(ids.T.astype(F32), ((0, 2), (0, 0))) + jnp.pad(coefs.T, ((2, 0), (0, 0)))
    to_x, by_x, to_y, by_y = spread(own, keep, got, out_grad)
    mine, _ = lax.optimization_barrier((out_grad, by_x))
    far = [along(mine, k) for k in range(1, nz)]
    a, a_send, b, b_send, near_by, metas = first_sum(
        out_grad, own, by_x, send(to_x, 0, 1), by_y, send(to_y, 2, 0)
    )
    other = send(near_by, 1, 0)
    far = stack(far, a)
    *terms, cross = second_sum(own, a, b, send(a_send, 2, 0), send(b_send, 0, 1))
    sums = [terms[0]] + [along(terms[k], k) for k in range(1, nz)]

    far_y, far_x = send(far, 2, 0), send(far, 0, 1)
    low, high = send(far_x[: nz // 2], 2, 0), send(far_y[nz // 2 :], 0, 1)
    here = backward_here(
        hidden, down_weight, metas, send(metas, 1, 0), (near_by, other), (cross, send(cross, 1, 0)), (sums[1], sums[-1])
    )
    parts = [far, far_x, far_y, low, high]
    after = [None, None, None, here[0], None]
    grads = parts + [
        send(p if held is None else lax.optimization_barrier((p, held))[0], 1, 0) for p, held in zip(parts, after)
    ]
    hid_grad, down_grad, mark = backward(hidden, down_weight, here, grads, ())
    mixed = last_sum(sums, mark)
    return (mixed, hid_grad, down_grad)


def local(hidden, down_weight, expert_ids, combine, out_grad):
    dp_count, cut_count = lax.axis_size("dp"), lax.axis_size("cuts")
    few = dp_count == 4 and cut_count % 4 == 0 and expert_ids.shape[0] <= out_grad.shape[1] and dp_count * expert_ids.shape[0] <= 2 * hidden.shape[1]
    return (shared if few else routed)(hidden, down_weight, expert_ids, combine, out_grad)


def solution(mesh):
    return jax.shard_map(
        local,
        mesh=mesh,
        in_specs=(
            P("dp", None, "cuts"),
            P("dp", "cuts", None),
            P("dp", None),
            P("dp", None),
            P("dp", "cuts"),
        ),
        out_specs=(P("dp", "cuts"), P("dp", None, "cuts"), P("dp", "cuts", None)),
        check_vma=False,
    )
```

```python
import functools

import jax
import jax.numpy as jnp
from jax import lax
from jax.experimental import pallas as pl
from jax.experimental.pallas import tpu as pltpu
from jax.sharding import PartitionSpec as P

BF, F32 = jnp.bfloat16, jnp.float32


def routed(hidden, down_weight, expert_ids, combine, out_grad):
    dp_count = lax.axis_size("dp")
    tok_rows = expert_ids.shape[0]
    capacity = 2 * tok_rows // dp_count
    slot_count = dp_count * capacity
    feat_share = out_grad.shape[1]
    width = down_weight.shape[2]
    flat_ids = expert_ids.reshape(-1)
    labels = jnp.arange(dp_count, dtype=jnp.int32)
    onehot = (flat_ids[:, None] == labels[None, :]).astype(jnp.int32)
    pair_rank = jnp.sum((jnp.cumsum(onehot, axis=0) - 1) * onehot, axis=1)
    inside = flat_ids < dp_count
    target = jnp.where(inside, flat_ids * capacity + pair_rank, dp_count * capacity)
    weights = combine.reshape(-1)
    full_grad = lax.all_gather(out_grad, "cuts", axis=1, tiled=True)
    scaled = (weights[:, None] * jnp.repeat(full_grad, 2, axis=0).astype(F32)).astype(BF)
    outgoing = jnp.zeros((dp_count * capacity, width), BF).at[target].set(scaled, mode="drop")
    incoming = lax.all_to_all(
        outgoing.reshape(dp_count, capacity, width), "dp", split_axis=0, concat_axis=0, tiled=True
    )
    grad_rows = incoming.reshape(slot_count, width)
    hidden_rows = hidden[0]
    weight = down_weight[0]
    own_share = lax.psum_scatter(
        lax.dot_general(weight, hidden_rows, (((0,), (1,)), ((), ())), preferred_element_type=F32),
        "cuts",
        scatter_dimension=0,
        tiled=True,
    )
    hid_grad = lax.dot_general(
        grad_rows, weight, (((1,), (1,)), ((), ())), preferred_element_type=F32
    ).astype(BF)
    down_grad = lax.dot_general(
        hidden_rows, grad_rows, (((0,), (0,)), ((), ())), preferred_element_type=F32
    ).astype(BF)
    returned = lax.all_to_all(
        own_share.astype(BF), "dp", split_axis=1, concat_axis=1, tiled=True
    )
    pick_index = jnp.minimum(target, dp_count * capacity - 1)
    picked = jnp.take(returned, pick_index, axis=1).astype(F32)
    pair_coef = jnp.where(inside, weights, jnp.zeros_like(weights))
    summed = jnp.sum((picked * pair_coef[None, :]).reshape(feat_share, tok_rows, 2), axis=2)
    mixed = summed.T.astype(BF)
    return (mixed, hid_grad[None], down_grad[None])


def routing(meta, expert, capacity):
    tok = meta.shape[1]
    label = jnp.full((1, tok), expert).astype(F32)
    first, second = meta[0:1] == label, meta[1:2] == label
    named = jnp.where(first, 1.0, jnp.where(second, 1.0, 0.0))
    weight = jnp.where(first, meta[2:3], jnp.where(second, meta[3:4], 0.0))
    earlier = lax.broadcasted_iota(jnp.int32, (tok, tok), 0) < lax.broadcasted_iota(
        jnp.int32, (tok, tok), 1
    )
    rank = jnp.dot(
        jnp.broadcast_to(named, (8, tok)).astype(BF),
        jnp.where(earlier, 1.0, 0.0).astype(BF),
        preferred_element_type=F32,
    )[0:1]
    slot = lax.broadcasted_iota(jnp.int32, (capacity, tok), 0).astype(F32)
    hot = jnp.where(slot == rank, named, 0.0)
    return hot, weight


def forward_kernel(nz, capacity, hidden_ref, weight_ref, keep_ref, send_ref, *scratch):
    held, wide, part, rows, sems = scratch
    me = lax.axis_index("dp")
    feat = keep_ref.shape[-1]
    ff = wide.shape[0]
    mid = ff // 2
    first = pltpu.make_async_copy(hidden_ref.at[0], held, sems.at[0])
    low = pltpu.make_async_copy(weight_ref.at[0, pl.ds(0, mid)], wide.at[pl.ds(0, mid)], sems.at[1])
    high = pltpu.make_async_copy(weight_ref.at[0, pl.ds(mid, mid)], wide.at[pl.ds(mid, mid)], sems.at[2])
    for copy in (first, low, high):
        copy.start()
    first.wait()
    low.wait()
    for z in range(nz):
        columns = slice(2 * z * feat, 2 * (z + 1) * feat)
        part[z] = jnp.dot(held[:, :mid], wide[:mid, columns], preferred_element_type=F32)
    high.wait()
    for z in range(nz):
        columns = slice(2 * z * feat, 2 * (z + 1) * feat)
        rest = jnp.dot(held[:, mid:], wide[mid:, columns], preferred_element_type=F32)
        rows[...] = (part[z] + rest).astype(BF)
        for dy in range(2):
            for dc, out in ((0, keep_ref), (1, send_ref)):
                at = pl.multiple_of((me ^ (2 * dy + dc)) * capacity, capacity)
                for x in range(2):
                    out[z, x, dy] = rows[pl.ds(at, capacity), x * feat : (x + 1) * feat]


def forward(hidden, weight, feat, dp_count):
    _, slots, ff = hidden.shape
    width = weight.shape[2]
    nz, capacity = width // (2 * feat), slots // dp_count
    part = jax.ShapeDtypeStruct((nz, 2, 2, capacity, feat), BF)
    hbm, vmem = pl.BlockSpec(memory_space=pltpu.HBM), pl.BlockSpec(memory_space=pltpu.VMEM)
    return pl.pallas_call(
        functools.partial(forward_kernel, nz, capacity),
        in_specs=[hbm] * 2,
        out_specs=[vmem] * 2,
        out_shape=[part, part],
        scratch_shapes=[
            pltpu.VMEM((slots, ff), BF),
            pltpu.VMEM((ff, width), BF),
            pltpu.VMEM((nz, slots, 2 * feat), F32),
            pltpu.VMEM((slots, 2 * feat), BF),
            pltpu.SemaphoreType.DMA((3,)),
        ],
        compiler_params=pltpu.CompilerParams(vmem_limit_bytes=50 << 20),
        cost_estimate=pl.CostEstimate(
            flops=2 * slots * ff * width, bytes_accessed=2 * (ff * width + slots * (ff + width)), transcendentals=0
        ),
        name="forward_rows",
    )(hidden, weight)


def by_token(meta, experts, capacity):
    tok = meta.shape[1]
    table = []
    for expert in experts:
        hot, weight = routing(meta, expert, capacity)
        table.append((hot.astype(BF), jnp.broadcast_to(weight, (tok, tok)).T[:, 0:1]))

    def add_up(first, second):
        terms = [
            lax.dot_general(hot, rows, (((0,), (0,)), ((), ())), preferred_element_type=F32) * weight
            for (hot, weight), rows in zip(table, (first, second))
        ]
        return terms[0] + terms[1]

    return add_up


def spread_kernel(nz, capacity, meta_ref, keep_ref, got_ref, grad_ref, to_x, by_x, to_y, by_y, split):
    me, x = lax.axis_index("dp"), lax.axis_index("cuts") % 2
    half = nz // 2
    tok = grad_ref.shape[0]
    to_x[nz] = grad_ref[...]
    to_y[nz * tok : (nz + 1) * tok] = grad_ref[...]
    rest = meta_ref[...]
    count = rest.shape[0]
    split[...] = jnp.zeros_like(split)
    for i in range(3):
        piece = rest.astype(BF).astype(F32)
        split[count * i : count * (i + 1)] = piece
        rest = rest - piece
    to_y[(nz + 1) * tok :, :tok] = split[...].astype(BF)
    add_up = by_token(meta_ref[...], (me, me ^ 1), capacity)
    for z in range(half):
        to_x[z] = add_up(keep_ref[z, x ^ 1, 0], got_ref[z, x ^ 1, 0]).astype(BF)
        by_x[z] = add_up(keep_ref[z, x, 0], got_ref[z, x, 0])
        to_x[half + z, :capacity] = keep_ref[z, x ^ 1, 1]
        to_x[half + z, capacity:] = got_ref[z, x ^ 1, 1]
        by_x[half + z, :capacity] = keep_ref[z, x, 1].astype(F32)
        by_x[half + z, capacity:] = got_ref[z, x, 1].astype(F32)
        for dx in range(2):
            by_y[half * dx + z] = add_up(keep_ref[half + z, x ^ dx, 0], got_ref[half + z, x ^ dx, 0])
            at = (half * dx + z) * tok
            to_y[at : at + capacity] = keep_ref[half + z, x ^ dx, 1]
            to_y[at + capacity : at + tok] = got_ref[half + z, x ^ dx, 1]


def spread(meta, keep, got, grad):
    nz, _, _, capacity, _ = keep.shape
    tok, feat = grad.shape
    kept = jax.ShapeDtypeStruct((nz, tok, feat), F32)
    return pl.pallas_call(
        functools.partial(spread_kernel, nz, capacity),
        out_shape=[
            jax.ShapeDtypeStruct((nz + 1, tok, feat), BF),
            kept,
            jax.ShapeDtypeStruct(((nz + 1) * tok + 16, feat), BF),
            kept,
        ],
        scratch_shapes=[pltpu.VMEM((16, tok), F32)],
        compiler_params=pltpu.CompilerParams(vmem_limit_bytes=24 << 20),
        cost_estimate=pl.CostEstimate(
            flops=16 * tok * capacity * nz * feat, bytes_accessed=24 * tok * nz * feat, transcendentals=0
        ),
        name="spread_rows",
    )(meta, keep, got, grad)


def first_sum_kernel(half, grad_ref, meta_ref, x_kept, x_got, y_kept, y_got, *refs):
    x_keep, x_send, y_keep, y_send, near_by, metas = refs
    me, tok, count = lax.axis_index("dp"), x_kept.shape[1], meta_ref.shape[0]
    capacity, mid = tok // 2, tok // 2
    own = 2 * half * tok
    near_by[0] = grad_ref[...]
    near_by[1] = x_got[2 * half]
    near_by[2] = y_got[own : own + tok]
    x_send[half * tok :] = x_got[2 * half, :mid]
    y_send[half * tok :] = y_got[own + mid : own + tok]
    split = y_got[own + tok :, :tok].astype(F32)
    metas[0] = meta_ref[...]
    metas[1] = split[:count] + split[count : 2 * count] + split[2 * count : 3 * count]
    add_up = by_token(meta_ref[...], (me ^ 2, me ^ 3), capacity)

    def come(place):
        at = place * tok
        return add_up(y_got[at : at + capacity], y_got[at + capacity : at + tok])

    for z in range(half):
        here = slice(z * tok, (z + 1) * tok)
        x_keep[z] = x_kept[z] + x_got[z].astype(F32)
        x_send[here] = (x_kept[half + z] + x_got[half + z].astype(F32)).astype(BF)
        y_keep[z] = y_kept[z] + come(z)
        y_send[here] = (y_kept[half + z] + come(half + z)).astype(BF)


def first_sum(grad, meta, x_kept, x_got, y_kept, y_got):
    nz, tok, feat = x_kept.shape
    half = nz // 2
    shapes = [
        jax.ShapeDtypeStruct((half, tok, feat), F32),
        jax.ShapeDtypeStruct((half * tok + tok // 2, feat), BF),
    ]
    return pl.pallas_call(
        functools.partial(first_sum_kernel, half),
        out_shape=shapes
        + shapes
        + [
            jax.ShapeDtypeStruct((3, tok, feat), BF),
            jax.ShapeDtypeStruct((2, *meta.shape), F32),
        ],
        compiler_params=pltpu.CompilerParams(vmem_limit_bytes=16 << 20),
        cost_estimate=pl.CostEstimate(flops=1000_000_000, bytes_accessed=0, transcendentals=0),
        name="first_sum",
    )(grad, meta, x_kept, x_got, y_kept, y_got)


def stack_kernel(_, *refs):
    for k, ref in enumerate(refs[:-1]):
        refs[-1][k] = ref[...]


def stack(parts, after):
    vmem = pl.BlockSpec(memory_space=pltpu.VMEM)
    return pl.pallas_call(
        stack_kernel,
        in_specs=[pl.BlockSpec(memory_space=pl.ANY)] + [vmem] * len(parts),
        out_specs=vmem,
        out_shape=jax.ShapeDtypeStruct((len(parts), *parts[0].shape), BF),
        compiler_params=pltpu.CompilerParams(vmem_limit_bytes=16 << 20),
        cost_estimate=pl.CostEstimate(flops=1000_000_000, bytes_accessed=0, transcendentals=0),
        name="stack_blocks",
    )(after, *parts)


def second_sum_kernel(nz, meta_ref, x_kept, y_kept, by_y, by_x, *refs):
    outs, cross, total = refs[:nz], refs[nz], refs[nz + 1]
    me, z, half = lax.axis_index("dp"), lax.axis_index("cuts") // 2, nz // 2
    tok = x_kept.shape[1]
    capacity, mid = tok // 2, tok // 2
    cross[:mid] = by_y[half * tok :]
    cross[mid:] = by_x[half * tok :]
    add_up = by_token(meta_ref[...], (me ^ 2, me ^ 3), capacity)
    for i in range(half):
        at = i * tok
        total[i] = x_kept[i] + add_up(by_y[at : at + capacity], by_y[at + capacity : at + tok])
        total[half + i] = y_kept[i] + by_x[at : at + tok].astype(F32)
    for k in range(nz):
        outs[k][...] = total[lax.rem(z + k, nz)].astype(outs[k].dtype)


def second_sum(meta, x_kept, y_kept, by_y, by_x):
    half, tok, feat = x_kept.shape
    nz = 2 * half
    return pl.pallas_call(
        functools.partial(second_sum_kernel, nz),
        out_shape=[jax.ShapeDtypeStruct((tok, feat), F32 if k == 0 else BF) for k in range(nz)]
        + [jax.ShapeDtypeStruct((tok, feat), BF)],
        scratch_shapes=[pltpu.VMEM((nz, tok, feat), F32)],
        compiler_params=pltpu.CompilerParams(vmem_limit_bytes=16 << 20),
        cost_estimate=pl.CostEstimate(flops=1000_000_000, bytes_accessed=0, transcendentals=0),
        name="second_sum",
    )(meta, x_kept, y_kept, by_y, by_x)


def put(rows_ref, hots, cols, dx, q, grads):
    capacity, feat = hots.shape[1], grads.shape[1]
    lane = pl.multiple_of((lax.axis_index("cuts") % 2 ^ dx) * feat, feat)
    at = pl.multiple_of((lax.axis_index("dp") ^ q) * capacity, capacity)
    picked = jnp.dot(hots[q], grads, preferred_element_type=F32)
    rows_ref[pl.ds(at, capacity), pl.ds(lane, feat)] = (picked * cols[q][:, 0:1]).astype(BF)


def columns(nz, k, feat):
    z = lax.rem(lax.axis_index("cuts") // 2 - k + nz, nz)
    return pl.ds(pl.multiple_of(z * 2 * feat, 2 * feat), 2 * feat)


def times_transposed(rows, weight):
    return lax.dot_general(rows, weight, (((1,), (1,)), ((), ())), preferred_element_type=F32)


def backward_here_kernel(nz, hidden_ref, weight_ref, metas, other_metas, *refs):
    grads, (part, down_out, turned, hots, cols), (made, rows_ref, sem) = refs[:4], refs[-8:-3], refs[-3:]
    me, capacity, feat = lax.axis_index("dp"), hots.shape[1], rows_ref.shape[1] // 2
    for dy in range(2):
        for dc, ref in enumerate((metas, other_metas)):
            hot, weight = routing(ref[dy], me, capacity)
            hots[2 * dy + dc] = hot.astype(BF)
            cols[2 * dy + dc] = jnp.broadcast_to(jnp.sum(hot * weight, axis=1, keepdims=True), cols.shape[1:])
    turned[...] = hidden_ref[0].T
    for dc in range(2):
        for j in range(4):
            put(rows_ref, hots, cols, j % 2, 2 * (j // 2) + dc, grads[dc][j] if j < 3 else grads[2 + dc][...])
    rows, column = rows_ref[...], columns(nz, 0, feat)
    mid, copies = made.shape[0] // 2, []
    for i in range(2):
        upper = slice(i * mid, (i + 1) * mid)
        made[upper] = jnp.dot(turned[upper], rows, preferred_element_type=F32).astype(BF)
        strip = pl.ds(i * mid, mid)
        copies.append(pltpu.make_async_copy(made.at[strip], down_out.at[0, strip, column], sem.at[i]))
        copies[i].start()
    part[...] = times_transposed(rows, weight_ref[0, :, column])
    for copy in copies:
        copy.wait()


def backward_here(hidden, weight, metas, other_metas, near_by, cross, after=()):
    _, slots, ff = hidden.shape
    tok, feat = near_by[0].shape[1:]
    capacity = slots // 4
    anywhere, vmem = pl.BlockSpec(memory_space=pl.ANY), pl.BlockSpec(memory_space=pltpu.VMEM)
    return pl.pallas_call(
        functools.partial(backward_here_kernel, weight.shape[2] // (2 * feat)),
        in_specs=[vmem] * 8 + [anywhere] * len(after),
        out_specs=[vmem, anywhere, vmem, vmem, vmem],
        scratch_shapes=[
            pltpu.VMEM((ff, 2 * feat), BF),
            pltpu.VMEM((slots, 2 * feat), BF),
            pltpu.SemaphoreType.DMA((2,)),
        ],
        out_shape=[
            jax.ShapeDtypeStruct((slots, ff), F32),
            jax.ShapeDtypeStruct(weight.shape, BF),
            jax.ShapeDtypeStruct((ff, slots), BF),
            jax.ShapeDtypeStruct((4, capacity, tok), BF),
            jax.ShapeDtypeStruct((4, capacity, 128), F32),
        ],
        compiler_params=pltpu.CompilerParams(vmem_limit_bytes=16 << 20),
        cost_estimate=pl.CostEstimate(flops=2000_000_000, bytes_accessed=0, transcendentals=0),
        name="backward_here",
    )(hidden, weight, metas, other_metas, *near_by, *cross, *after)


def backward_kernel(nz, weight_ref, part_ref, turned, hots, cols, *refs):
    grads, (hid_out, down_out, mark), (made, rows_ref, total, done, sems) = (refs[:5], refs[5:10]), refs[-8:-5], refs[-5:]
    feat = rows_ref.shape[1] // 2
    mark[...] = jnp.zeros_like(mark)
    leaving = []
    for k in range(1, nz):
        for dc in range(2):
            far, far_x, far_y, low, high = grads[dc]
            count = low.shape[0]
            cross = low[k - 1] if k <= count else high[k - 1 - count]
            for j, rows in enumerate((far[k - 1], far_x[k - 1], far_y[k - 1], cross)):
                put(rows_ref, hots, cols, j % 2, 2 * (j // 2) + dc, rows)
        rows, column = rows_ref[...], columns(nz, k, feat)
        if k > 2:
            leaving.pop(0).wait()
        made[k % 2] = jnp.dot(turned[...], rows, preferred_element_type=F32).astype(BF)
        leaving.append(pltpu.make_async_copy(made.at[k % 2], down_out.at[0, :, column], sems.at[k % 2]))
        leaving[-1].start()
        part = (part_ref if k == 1 else total)[...] + times_transposed(rows, weight_ref[0, :, column])
        if k < nz - 1:
            total[...] = part
        else:
            done[...] = part.astype(BF)
            leaving.append(pltpu.make_async_copy(done, hid_out.at[0], sems.at[2]))
            leaving[-1].start()
    for copy in leaving:
        copy.wait()


def backward(hidden, weight, here, grads, after=()):
    part, down, turned, hots, cols = here
    feat = grads[0].shape[2]
    _, slots, ff = hidden.shape
    anywhere, vmem = pl.BlockSpec(memory_space=pl.ANY), pl.BlockSpec(memory_space=pltpu.VMEM)
    return pl.pallas_call(
        functools.partial(backward_kernel, weight.shape[2] // (2 * feat)),
        in_specs=[vmem] * 15 + [anywhere] * (1 + len(after)),
        out_specs=[anywhere, anywhere, vmem],
        scratch_shapes=[
            pltpu.VMEM((2, ff, 2 * feat), BF),
            pltpu.VMEM((slots, 2 * feat), BF),
            pltpu.VMEM((slots, ff), F32),
            pltpu.VMEM((slots, ff), BF),
            pltpu.SemaphoreType.DMA((3,)),
        ],
        out_shape=[
            jax.ShapeDtypeStruct(hidden.shape, BF),
            jax.ShapeDtypeStruct(weight.shape, BF),
            jax.ShapeDtypeStruct((8, 128), F32),
        ],
        input_output_aliases={15: 1},
        compiler_params=pltpu.CompilerParams(vmem_limit_bytes=32 << 20),
        cost_estimate=pl.CostEstimate(flops=100_000_000, bytes_accessed=0, transcendentals=0),
        name="backward_rows",
    )(weight, part, turned, hots, cols, *grads, down, *after)


def last_sum_kernel(_, first_ref, *refs):
    total = first_ref[...]
    for ref in refs[:-1]:
        total = total + ref[...].astype(F32)
    refs[-1][...] = total.astype(BF)


def last_sum(parts, after):
    vmem = pl.BlockSpec(memory_space=pltpu.VMEM)
    return pl.pallas_call(
        last_sum_kernel,
        in_specs=[pl.BlockSpec(memory_space=pl.ANY)] + [vmem] * len(parts),
        out_specs=vmem,
        out_shape=jax.ShapeDtypeStruct(parts[0].shape, BF),
        compiler_params=pltpu.CompilerParams(vmem_limit_bytes=16 << 20),
        cost_estimate=pl.CostEstimate(flops=1000_000_000, bytes_accessed=0, transcendentals=0),
        name="last_sum",
    )(after, *parts)


def shared(hidden, down_weight, expert_ids, combine, out_grad):
    dp_count, cut_count = lax.axis_size("dp"), lax.axis_size("cuts")
    nz = cut_count // 2
    feat = out_grad.shape[1]

    def send(value, dp_flip, cut_flip):
        pairs = [
            (d * cut_count + c, (d ^ dp_flip) * cut_count + (c ^ cut_flip))
            for d in range(dp_count)
            for c in range(cut_count)
        ]
        return lax.ppermute(value, ("dp", "cuts"), pairs)

    def along(value, k):
        return lax.ppermute(value, "cuts", [(c, (c + 2 * k) % cut_count) for c in range(cut_count)])

    keep, away = forward(hidden, down_weight, out_grad.shape[1], dp_count)
    got = send(away, 1, 0)
    ids, coefs, _ = lax.optimization_barrier((expert_ids, combine, keep))
    own = jnp.pad(ids.T.astype(F32), ((0, 2), (0, 0))) + jnp.pad(coefs.T, ((2, 0), (0, 0)))
    to_x, by_x, to_y, by_y = spread(own, keep, got, out_grad)
    mine, _ = lax.optimization_barrier((out_grad, by_x))
    far = [along(mine, k) for k in range(1, nz)]
    a, a_send, b, b_send, near_by, metas = first_sum(
        out_grad, own, by_x, send(to_x, 0, 1), by_y, send(to_y, 2, 0)
    )
    other = send(near_by, 1, 0)
    far = stack(far, a)
    *terms, cross = second_sum(own, a, b, send(a_send, 2, 0), send(b_send, 0, 1))
    sums = [terms[0]] + [along(terms[k], k) for k in range(1, nz)]

    far_y, far_x = send(far, 2, 0), send(far, 0, 1)
    low, high = send(far_x[: nz // 2], 2, 0), send(far_y[nz // 2 :], 0, 1)
    here = backward_here(
        hidden, down_weight, metas, send(metas, 1, 0), (near_by, other), (cross, send(cross, 1, 0)), (sums[1], sums[-1])
    )
    parts = [far, far_x, far_y, low, high]
    after = [None, None, None, here[0], None]
    grads = parts + [
        send(p if held is None else lax.optimization_barrier((p, held))[0], 1, 0) for p, held in zip(parts, after)
    ]
    hid_grad, down_grad, mark = backward(hidden, down_weight, here, grads, ())
    mixed = last_sum(sums, mark)
    return (mixed, hid_grad, down_grad)


def local(hidden, down_weight, expert_ids, combine, out_grad):
    dp_count, cut_count = lax.axis_size("dp"), lax.axis_size("cuts")
    few = dp_count == 4 and cut_count % 4 == 0 and expert_ids.shape[0] <= out_grad.shape[1] and dp_count * expert_ids.shape[0] <= 2 * hidden.shape[1]
    return (shared if few else routed)(hidden, down_weight, expert_ids, combine, out_grad)


def solution(mesh):
    return jax.shard_map(
        local,
        mesh=mesh,
        in_specs=(
            P("dp", None, "cuts"),
            P("dp", "cuts", None),
            P("dp", None),
            P("dp", None),
            P("dp", "cuts"),
        ),
        out_specs=(P("dp", "cuts"), P("dp", None, "cuts"), P("dp", "cuts", None)),
        check_vma=False,
    )
```
